512 devices in a mesh: ctx: 32 (over z, core), tp: 16 (over x, y).
Axes of the slice: x: 4, y: 4, z: 16, core: 2. Of those that a mesh axis runs over, the one named last changes fastest.
Arguments:
- teacher_span: bfloat16 [512, 8192], P('ctx', 'tp'), may hold values from -20 to 20
- teacher_context: bfloat16 [16384, 8192], P(('ctx', 'tp')), may hold values from -16 to 16
- student_span: bfloat16 [512, 2560], P('ctx', 'tp'), may hold values from -28 to 28
- student_context: bfloat16 [16384, 2560], P(('ctx', 'tp')), may hold values from -20 to 20
- query_weights: float32 [512], replicated, may hold values from 0.25 to 4
Outputs:
- grad_span: float32 [512, 2560], P('ctx', 'tp')
- grad_context: float32 [16384, 2560], P(('ctx', 'tp'))
The draws below stay inside these ranges and needn't reach their ends.
All inputs are finite; a program needn't handle non-finite values.
Results may differ from the reference program's by a relative error of at most 0.0022.
Values may be sent and summed in bfloat16 or wider, within the bound.
No kernel may reach another device: no remote copies, remote signals or barrier semaphores. Data moves between devices by JAX's collectives and lax.ppermute only.
A program may use at most 64 MiB of HBM per device.

```python
import math
import jax
import jax.numpy as jnp
from jax import lax

DT = 8192
DS = 2560
HEADS = 64
QN = 512
TH = 128
SH = 40
KEYS = 16384


def column_group(key, width, salt):
    return jax.random.randint(jax.random.fold_in(key, salt), (width,), 0, 2).astype(jnp.float32)


def base_rows(key, rows, width, limit):
    return jnp.clip(jax.random.normal(key, (rows, width), jnp.float32), -limit, limit)


def draw_teacher_span(key, part):
    group = column_group(key, DT, 91)
    key = jax.random.fold_in(key, 1)
    values = base_rows(key, QN, DT, 4.0) * (1.0 + 4.0 * group)[None, :]
    return values.astype(jnp.bfloat16)


def draw_teacher_context(key, part):
    group = column_group(key, DT, 91)
    key = jax.random.fold_in(key, 2)
    values = base_rows(key, KEYS, DT, 5.0) * (1.0 - 0.9 * group)[None, :]
    return values.astype(jnp.bfloat16)


def draw_student_span(key, part):
    group = column_group(key, DS, 92)
    key = jax.random.fold_in(key, 3)
    values = base_rows(key, QN, DS, 4.0) * (1.0 + 6.0 * group)[None, :]
    return values.astype(jnp.bfloat16)


def draw_student_context(key, part):
    group = column_group(key, DS, 92)
    key = jax.random.fold_in(key, 4)
    values = base_rows(key, KEYS, DS, 5.0) * (1.0 - 0.9 * group)[None, :]
    return values.astype(jnp.bfloat16)


def setup_inputs(seed: int = 0) -> dict:
    streams_of = jax.random.split(jax.random.key(seed), 6)
    return {
        "teacher_span": draw_teacher_span(jax.random.fold_in(streams_of[5], 71), 0),
        "teacher_context": draw_teacher_context(jax.random.fold_in(streams_of[5], 71), 0),
        "student_span": draw_student_span(jax.random.fold_in(streams_of[5], 71), 0),
        "student_context": draw_student_context(jax.random.fold_in(streams_of[5], 71), 0),
        "query_weights": jnp.clip(jnp.exp(jax.random.uniform(streams_of[4], (QN,), jnp.float32, math.log(0.25), math.log(4.0))), 0.25, 4.0),
    }


def reference(teacher_span, teacher_context, student_span, student_context, query_weights):
    teach_rows = teacher_span.reshape(QN, HEADS, TH).transpose(1, 0, 2)
    teach_keys = teacher_context.reshape(KEYS, HEADS, TH).transpose(1, 0, 2)
    stud_rows = student_span.reshape(QN, HEADS, SH).transpose(1, 0, 2)
    stud_keys = student_context.reshape(KEYS, HEADS, SH).transpose(1, 0, 2)
    row_coef = (math.sqrt(KEYS) * query_weights.astype(jnp.float32))[:, None]

    def one_head(pieces):
        teach_q, teach_k, stud_q, stud_k = pieces
        teach_score = jnp.dot(teach_q, teach_k.T, preferred_element_type=jnp.float32) / math.sqrt(TH)
        stud_score = jnp.dot(stud_q, stud_k.T, preferred_element_type=jnp.float32) / math.sqrt(SH)
        teach_prob = jax.nn.softmax(teach_score, axis=-1)
        stud_prob = jax.nn.softmax(stud_score, axis=-1)
        grad_score = (row_coef * (stud_prob - teach_prob)).astype(jnp.bfloat16)
        grad_query = jnp.dot(grad_score, stud_k, preferred_element_type=jnp.float32) / math.sqrt(SH)
        grad_key = jnp.dot(grad_score.T, stud_q, preferred_element_type=jnp.float32) / math.sqrt(SH)
        return (grad_query, grad_key)
    grad_query, grad_key = lax.map(one_head, (teach_rows, teach_keys, stud_rows, stud_keys))
    grad_span = grad_query.transpose(1, 0, 2).reshape(QN, DS)
    grad_context = grad_key.transpose(1, 0, 2).reshape(KEYS, DS)
    return (grad_span, grad_context)
```

```python
import functools
import math

import jax
import jax.numpy as jnp
from jax import lax
from jax.experimental import pallas as pl
from jax.experimental.pallas import tpu as pltpu
from jax.sharding import Mesh, PartitionSpec as P

TH = 128
SH = 40
CORES = 2
NEAR = 2
LANES = 128
HALF = LANES // 2
LOG2E = math.log2(math.e)
F32 = jnp.float32
BF16 = jnp.bfloat16


def side_by_side(low, high):
    gap = jnp.zeros((low.shape[0], HALF - SH), low.dtype)
    return jnp.concatenate([low, gap, high, gap], axis=1)


def pack(side_ref, tq_hbm, tk_hbm, sq_hbm, sk_hbm, keys_hbm, kept_ref, given_ref,
         tq_ref, tk_ref, sq_ref, sk_ref, keys_ref, sems):
    heads, tokens, half = keys_hbm.shape[0], tk_hbm.shape[0], tk_hbm.shape[0] // 2
    fetches = [
        pltpu.make_async_copy(source, target, sems.at[number])
        for number, (source, target) in enumerate(
            [(tq_hbm, tq_ref), (sq_hbm, sq_ref), (sk_hbm, sk_ref), (tk_hbm, tk_ref)]
        )
    ]
    for copy in fetches:
        copy.start()
    rows = tq_ref.shape[0]

    def fill(out_ref, second):
        teach = [tq_ref[:, head * TH : (head + 1) * TH] for head in range(NEAR * CORES)]
        out_ref[:rows, :] = jnp.where(second, teach[1], teach[0])
        out_ref[rows : 2 * rows, :] = jnp.where(second, teach[2], teach[3])
        stud = [sq_ref[:, head * SH : (head + 1) * SH] for head in range(NEAR * CORES)]
        out_ref[2 * rows :, :] = jnp.where(
            second, side_by_side(stud[1], stud[2]), side_by_side(stud[0], stud[3])
        )

    fetches[0].wait()
    fetches[1].wait()
    second = side_ref[0] == 1
    fill(kept_ref, second)
    fill(given_ref, jnp.logical_not(second))
    fetches[2].wait()
    for head in range(heads):
        part = sk_ref[:, head * SH : (head + 1) * SH]
        keys_ref[head, tokens:, :] = side_by_side(part[:half], part[half:])
    fetches[3].wait()
    group = heads // 4
    sends = []
    for start in range(0, heads, group):
        for head in range(start, start + group):
            keys_ref[head, :tokens, :] = tk_ref[:, head * TH : (head + 1) * TH]
        here = pl.ds(start, group)
        sends.append(
            pltpu.make_async_copy(keys_ref.at[here], keys_hbm.at[here], sems.at[4 + start // group])
        )
        sends[-1].start()
    for copy in sends:
        copy.wait()


def queries_of(near_ref, rows_ref):
    count, deep, lanes = rows_ref.shape
    own = deep // (NEAR + 1)
    near = near_ref[0]
    start = pl.multiple_of(near * own, own)
    teach = rows_ref[:, pl.ds(start, own), :].reshape(count * own, lanes)
    stud = rows_ref[:, NEAR * own :, :].reshape(count * own, lanes).astype(F32)
    turned = jnp.concatenate([stud[:, HALF:], stud[:, :HALF]], axis=1)
    low = lax.broadcasted_iota(jnp.int32, (1, lanes), 1) < HALF
    first = near == 0
    left = jnp.where(low, jnp.where(first, stud, turned), 0.0)
    right = jnp.where(low, 0.0, jnp.where(first, turned, stud))
    return teach, left.astype(BF16), right.astype(BF16)


def key_chunk(keys_ref, start, size):
    part = keys_ref[pl.ds(start, size)]
    own = part.shape[1] // 3
    flat = lambda block: block.reshape(size * own, LANES)
    return flat(part[:, :own]), flat(part[:, own : 2 * own]), flat(part[:, 2 * own :])


def scores_of(span, key):
    return lax.dot_general(key, span, (((1,), (1,)), ((), ())), preferred_element_type=F32)


def turn(array):
    return jnp.concatenate([array[..., HALF:], array[..., :HALF]], axis=-1)


def low_lanes(rank):
    shape = (1,) * (rank - 1) + (LANES,)
    return lax.broadcasted_iota(jnp.int32, shape, rank - 1) < HALF


def totals_kernel(chunk, near_ref, keys_ref, rows_ref, out_ref, span_ref, score_ref):
    teach_q, left_q, right_q = queries_of(near_ref, rows_ref)
    span_ref[0], span_ref[1], span_ref[2] = teach_q, left_q, right_q
    queries = teach_q.shape[0]
    steps = keys_ref.shape[0] // chunk
    scales = (LOG2E / math.sqrt(TH), LOG2E / math.sqrt(SH))

    def measure(index, tops):
        first, second, pack = key_chunk(keys_ref, index * chunk, chunk)
        here = pl.ds(index * first.shape[0], first.shape[0])
        found = []
        for kind, span, key in ((0, 0, first), (0, 0, second), (1, 1, pack), (1, 2, pack)):
            score = scores_of(span_ref[span], key)
            score_ref[len(found), here] = score
            found.append(jnp.max(score.reshape(-1, 8, queries), axis=0))
        return jnp.maximum(tops[0], jnp.maximum(found[0], found[1])), jnp.maximum(
            tops[1], jnp.maximum(found[2], found[3])
        )

    start = jnp.full((8, queries), -1e30, F32)
    tops = lax.fori_loop(0, steps, measure, (start, start), unroll=True)
    tops = [jnp.max(top, axis=0, keepdims=True) * scale for top, scale in zip(tops, scales)]

    def gather(index, state):
        sums, means = list(state[:2]), state[2]
        _, _, pack = key_chunk(keys_ref, index * chunk, chunk)
        here = pl.ds(index * pack.shape[0], pack.shape[0])
        low = low_lanes(2)
        none = jnp.zeros_like(pack)
        turned = turn(pack.astype(F32)).astype(BF16)
        keys = (
            jnp.where(low, pack, none),
            jnp.where(low, turned, none),
            jnp.where(low, none, turned),
            jnp.where(low, none, pack),
        )
        left, right = [], []
        for number in range(4):
            kind = number // 2
            prob = jnp.exp2(score_ref[number, here] * scales[kind] - tops[kind])
            sums[kind] = sums[kind] + jnp.sum(prob.reshape(-1, 8, queries), axis=0)
            high = prob.astype(BF16)
            left += [keys[number], keys[number]]
            right += [high, (prob - high.astype(F32)).astype(BF16)]
        means = means + lax.dot_general(
            jnp.concatenate(left, axis=0),
            jnp.concatenate(right, axis=0),
            (((0,), (0,)), ((), ())),
            preferred_element_type=F32,
        )
        return sums[0], sums[1], means

    none = jnp.zeros((8, queries), F32)
    state = lax.fori_loop(
        0, steps, gather, (none, none, jnp.zeros((LANES, queries), F32)), unroll=True
    )
    lines, columns = [], []
    for kind in range(2):
        total = jnp.sum(state[kind], axis=0, keepdims=True)
        log = tops[kind] + jnp.log2(total)
        lines += [log[:, k : k + LANES] for k in range(0, queries, LANES)]
        mean = state[2][kind * HALF : kind * HALF + SH] * (1.0 / total)
        columns += [mean, jnp.broadcast_to(log, (HALF - SH, queries))]
    groups, own = out_ref.shape[0], out_ref.shape[1] - 8
    out_ref[:, :own, :] = jnp.concatenate(columns, axis=0).T.reshape(groups, own, LANES)
    out_ref[:, own:, :] = jnp.broadcast_to(
        jnp.concatenate(lines, axis=0)[None], (groups, 8, LANES)
    )


def grads_kernel(
    chunk, near_ref, logs_ref, weights_ref, own_ref, keys_ref, rows_ref, key_ref, span_ref
):
    deep = logs_ref.shape[1] - 8
    logs = logs_ref[:, deep:, :]
    high = jnp.max(logs, axis=0)
    logs = high + jnp.log2(jnp.sum(jnp.exp2(logs - high[None]), axis=0))
    lines = logs.shape[0] // 2
    flat = lambda rows: jnp.concatenate([rows[k : k + 1] for k in range(lines)], axis=1)
    teach_log, stud_log = flat(logs[:lines]), flat(logs[lines:])
    weights = weights_ref[...]
    teach_q, left_q, right_q = queries_of(near_ref, rows_ref)
    span_ref[0], span_ref[1], span_ref[2] = teach_q, left_q, right_q
    own = key_ref.shape[1] // 2

    means = logs_ref[:, :deep, :]
    each = jnp.where(low_lanes(3), means[:, :, SH : SH + 1], means[:, :, HALF + SH : HALF + SH + 1])
    share = jnp.exp2(each - jnp.max(each, axis=0, keepdims=True))
    mean = jnp.sum(share * means, axis=0) / jnp.sum(share, axis=0)
    mean = (turn(mean) - mean) * own_ref[...] * (1.0 / math.sqrt(SH))
    rough = mean.astype(BF16).astype(F32)
    mean = jnp.where(low_lanes(2), rough, turn(mean - rough)).astype(BF16)
    for head in range(key_ref.shape[0]):
        start = head % (deep // own) * own
        key_ref[head, own:, :] = mean[start : start + own]

    def grad(teach_score, stud_score):
        teach = jnp.exp2(teach_score * (LOG2E / math.sqrt(TH)) - teach_log)
        stud = jnp.exp2(stud_score * (LOG2E / math.sqrt(SH)) - stud_log)
        return (weights * (stud - teach)).astype(BF16)

    def step(index, _):
        first, second, pack = key_chunk(keys_ref, index * chunk, chunk)
        left = grad(scores_of(span_ref[0], first), scores_of(span_ref[1], pack))
        right = grad(scores_of(span_ref[0], second), scores_of(span_ref[2], pack))
        mix = jnp.dot(left, span_ref[1], preferred_element_type=F32)
        mix = mix + jnp.dot(right, span_ref[2], preferred_element_type=F32)
        mix = (mix * (1.0 / math.sqrt(SH))).astype(key_ref.dtype)
        key_ref[pl.ds(index * chunk, chunk), :own, :] = mix.reshape(chunk, own, LANES)
        return 0

    lax.fori_loop(0, keys_ref.shape[0] // chunk, step, 0, unroll=True)


def unpack(tp_ref, in_ref, context_ref, span_ref):
    half = in_ref.shape[1] // 2
    group = 16
    for start in range(0, in_ref.shape[0], group):
        for side in range(2):
            parts = [
                in_ref[head, :half, side * HALF : side * HALF + SH].astype(F32)
                for head in range(start, start + group)
            ]
            context_ref[side * half : (side + 1) * half, start * SH : (start + group) * SH] = (
                jnp.concatenate(parts, axis=1)
            )
    near = NEAR * CORES
    rows = in_ref[pl.ds(tp_ref[0] * near, near), half:, :].astype(F32)
    rows = rows + turn(rows)
    span_ref[...] = jnp.concatenate([rows[head, :, :SH] for head in range(near)], axis=1)


def call(body, shapes, scratch=(), smem=0, raw=0, raw_out=0, flops=0, room=48):
    kinds = [pltpu.SMEM, pltpu.HBM, pltpu.VMEM]
    specs = lambda counts: [
        pl.BlockSpec(memory_space=kind) for kind, count in zip(kinds, counts) for _ in range(count)
    ]

    def run(*args):
        many = isinstance(shapes, (list, tuple))
        outs = specs((0, raw_out, (len(shapes) if many else 1) - raw_out))
        moved = sum(arg.size * arg.dtype.itemsize for arg in args)
        return pl.pallas_call(
            body,
            out_shape=shapes,
            in_specs=specs((smem, raw, len(args) - smem - raw)),
            out_specs=outs if many else outs[0],
            scratch_shapes=list(scratch),
            cost_estimate=pl.CostEstimate(flops=flops, bytes_accessed=moved, transcendentals=0),
            compiler_params=pltpu.CompilerParams(vmem_limit_bytes=room * 2**20),
        )(*args)

    return run


def on_device(teacher_span, teacher_context, student_span, student_context, query_weights):
    groups, tps = lax.axis_size("group"), lax.axis_size("tp")
    heads = tps * NEAR * CORES
    near = NEAR * CORES
    rows_own, tokens_own = teacher_span.shape[0], teacher_context.shape[0]
    half = tokens_own // 2
    queries = query_weights.shape[0]
    shape = jax.ShapeDtypeStruct

    def trade(array, axes):
        return lax.all_to_all(array, axes, split_axis=0, concat_axis=0, tiled=True)

    core, spot = lax.axis_index("core"), lax.axis_index("near").astype(jnp.int32).reshape(1)
    piece = shape(((NEAR + 1) * rows_own, LANES), BF16)
    keys, kept, given = call(
        pack,
        (shape((heads, 3 * half, LANES), BF16), piece, piece),
        scratch=[
            pltpu.VMEM(teacher_span.shape, BF16),
            pltpu.VMEM(teacher_context.shape, BF16),
            pltpu.VMEM(student_span.shape, BF16),
            pltpu.VMEM(student_context.shape, BF16),
            pltpu.VMEM((heads, 3 * half, LANES), BF16),
            pltpu.SemaphoreType.DMA((8,)),
        ],
        smem=1,
        raw=4,
        raw_out=1,
        room=62,
    )(
        (spot[0] ^ core).astype(jnp.int32).reshape(1),
        teacher_span,
        teacher_context,
        student_span,
        student_context,
    )
    other = lax.ppermute(given, "core", [(0, 1), (1, 0)])
    order = lambda first, second: jnp.stack(
        [part.reshape(NEAR + 1, rows_own, LANES) for part in (first, second)], axis=1
    )
    shard = jnp.where(core == 0, order(kept, other), order(other, kept))
    shard = shard.reshape(1, (NEAR + 1) * CORES * rows_own, LANES)
    keys = trade(keys, ("tp", "near", "core"))
    rows = lax.all_gather(
        shard,
        ("group", "near", "core"),
        axis=0,
        tiled=True,
        axis_index_groups=[
            [z * CORES + (z + side) % CORES for z in range(groups * NEAR)] for side in range(CORES)
        ],
    )

    spans = pltpu.VMEM((3, queries, LANES), BF16)
    deep = queries // groups
    logs = call(
        functools.partial(totals_kernel, 8),
        shape((groups, deep + 8, LANES), F32),
        scratch=[spans, pltpu.VMEM((4, heads * half, queries), F32)],
        smem=1,
        flops=2**31,
    )(spot, keys, rows)
    logs = trade(logs, "group")
    tokens_all = tokens_own * heads * groups
    weights = math.sqrt(tokens_all) * query_weights
    own = lax.dynamic_slice(weights, (lax.axis_index("group") * deep,), (deep,))
    own = jnp.broadcast_to(own[:, None], (deep, LANES))
    parts = call(
        functools.partial(grads_kernel, 8),
        shape((heads, 2 * half, LANES), BF16),
        scratch=[spans],
        smem=1,
        flops=2**30,
    )(spot, logs, weights.reshape(1, queries), own, keys, rows)
    parts = trade(parts, ("tp", "near", "core"))
    grad_context, grad_span = call(
        unpack, (shape((tokens_own, heads * SH), F32), shape((rows_own, near * SH), F32)), smem=1
    )(lax.axis_index("tp").astype(jnp.int32).reshape(1), parts)
    return (grad_span, grad_context)


def solution(mesh):
    ctx, tp = mesh.devices.shape
    split = Mesh(
        mesh.devices.reshape(ctx // (NEAR * CORES), NEAR, CORES, tp),
        ("group", "near", "core", "tp"),
    )
    rows = ("group", "near", "core")
    tokens = rows + ("tp",)
    placed = (P(rows, "tp"), P(tokens, None), P(rows, "tp"), P(tokens, None), P())
    return jax.shard_map(
        on_device,
        mesh=split,
        in_specs=placed,
        out_specs=(P(rows, "tp"), P(tokens, None)),
        check_vma=False,
    )
```

```python
import functools
import math

import jax
import jax.numpy as jnp
from jax import lax
from jax.experimental import pallas as pl
from jax.experimental.pallas import tpu as pltpu
from jax.sharding import Mesh, PartitionSpec as P

TH = 128
SH = 40
CORES = 2
NEAR = 2
LANES = 128
HALF = LANES // 2
LOG2E = math.log2(math.e)
F32 = jnp.float32
BF16 = jnp.bfloat16


def side_by_side(low, high):
    gap = jnp.zeros((low.shape[0], HALF - SH), low.dtype)
    return jnp.concatenate([low, gap, high, gap], axis=1)


def pack(side_ref, tq_hbm, tk_hbm, sq_hbm, sk_hbm, keys_hbm, kept_ref, given_ref,
         tq_ref, tk_ref, sq_ref, sk_ref, keys_ref, sems):
    heads, tokens, half = keys_hbm.shape[0], tk_hbm.shape[0], tk_hbm.shape[0] // 2
    fetches = [
        pltpu.make_async_copy(source, target, sems.at[number])
        for number, (source, target) in enumerate(
            [(tq_hbm, tq_ref), (sq_hbm, sq_ref), (sk_hbm, sk_ref), (tk_hbm, tk_ref)]
        )
    ]
    for copy in fetches:
        copy.start()
    rows = tq_ref.shape[0]

    def fill(out_ref, second):
        teach = [tq_ref[:, head * TH : (head + 1) * TH] for head in range(NEAR * CORES)]
        out_ref[:rows, :] = jnp.where(second, teach[1], teach[0])
        out_ref[rows : 2 * rows, :] = jnp.where(second, teach[2], teach[3])
        stud = [sq_ref[:, head * SH : (head + 1) * SH] for head in range(NEAR * CORES)]
        out_ref[2 * rows :, :] = jnp.where(
            second, side_by_side(stud[1], stud[2]), side_by_side(stud[0], stud[3])
        )

    fetches[0].wait()
    fetches[1].wait()
    second = side_ref[0] == 1
    fill(kept_ref, second)
    fill(given_ref, jnp.logical_not(second))
    fetches[2].wait()
    for head in range(heads):
        part = sk_ref[:, head * SH : (head + 1) * SH]
        keys_ref[head, tokens:, :] = side_by_side(part[:half], part[half:])
    fetches[3].wait()
    group = heads // 4
    sends = []
    for start in range(0, heads, group):
        for head in range(start, start + group):
            keys_ref[head, :tokens, :] = tk_ref[:, head * TH : (head + 1) * TH]
        here = pl.ds(start, group)
        sends.append(
            pltpu.make_async_copy(keys_ref.at[here], keys_hbm.at[here], sems.at[4 + start // group])
        )
        sends[-1].start()
    for copy in sends:
        copy.wait()


def queries_of(near_ref, rows_ref):
    count, deep, lanes = rows_ref.shape
    own = deep // (NEAR + 1)
    near = near_ref[0]
    start = pl.multiple_of(near * own, own)
    teach = rows_ref[:, pl.ds(start, own), :].reshape(count * own, lanes)
    stud = rows_ref[:, NEAR * own :, :].reshape(count * own, lanes).astype(F32)
    turned = jnp.concatenate([stud[:, HALF:], stud[:, :HALF]], axis=1)
    low = lax.broadcasted_iota(jnp.int32, (1, lanes), 1) < HALF
    first = near == 0
    left = jnp.where(low, jnp.where(first, stud, turned), 0.0)
    right = jnp.where(low, 0.0, jnp.where(first, turned, stud))
    return teach, left.astype(BF16), right.astype(BF16)


def key_chunk(keys_ref, start, size):
    part = keys_ref[pl.ds(start, size)]
    own = part.shape[1] // 3
    flat = lambda block: block.reshape(size * own, LANES)
    return flat(part[:, :own]), flat(part[:, own : 2 * own]), flat(part[:, 2 * own :])


def scores_of(span, key):
    return lax.dot_general(key, span, (((1,), (1,)), ((), ())), preferred_element_type=F32)


def turn(array):
    return jnp.concatenate([array[..., HALF:], array[..., :HALF]], axis=-1)


def low_lanes(rank):
    shape = (1,) * (rank - 1) + (LANES,)
    return lax.broadcasted_iota(jnp.int32, shape, rank - 1) < HALF


def totals_kernel(chunk, near_ref, keys_ref, rows_ref, out_ref, span_ref, score_ref):
    teach_q, left_q, right_q = queries_of(near_ref, rows_ref)
    span_ref[0], span_ref[1], span_ref[2] = teach_q, left_q, right_q
    queries = teach_q.shape[0]
    steps = keys_ref.shape[0] // chunk
    scales = (LOG2E / math.sqrt(TH), LOG2E / math.sqrt(SH))

    def measure(index, tops):
        first, second, pack = key_chunk(keys_ref, index * chunk, chunk)
        here = pl.ds(index * first.shape[0], first.shape[0])
        found = []
        for kind, span, key in ((0, 0, first), (0, 0, second), (1, 1, pack), (1, 2, pack)):
            score = scores_of(span_ref[span], key)
            score_ref[len(found), here] = score
            found.append(jnp.max(score.reshape(-1, 8, queries), axis=0))
        return jnp.maximum(tops[0], jnp.maximum(found[0], found[1])), jnp.maximum(
            tops[1], jnp.maximum(found[2], found[3])
        )

    start = jnp.full((8, queries), -1e30, F32)
    tops = lax.fori_loop(0, steps, measure, (start, start), unroll=2)
    tops = [jnp.max(top, axis=0, keepdims=True) * scale for top, scale in zip(tops, scales)]

    def gather(index, state):
        sums, means = list(state[:2]), state[2]
        _, _, pack = key_chunk(keys_ref, index * chunk, chunk)
        here = pl.ds(index * pack.shape[0], pack.shape[0])
        low = low_lanes(2)
        none = jnp.zeros_like(pack)
        turned = turn(pack.astype(F32)).astype(BF16)
        keys = (
            jnp.where(low, pack, none),
            jnp.where(low, turned, none),
            jnp.where(low, none, turned),
            jnp.where(low, none, pack),
        )
        left, right = [], []
        for number in range(4):
            kind = number // 2
            prob = jnp.exp2(score_ref[number, here] * scales[kind] - tops[kind])
            sums[kind] = sums[kind] + jnp.sum(prob.reshape(-1, 8, queries), axis=0)
            high = prob.astype(BF16)
            left += [keys[number], keys[number]]
            right += [high, (prob - high.astype(F32)).astype(BF16)]
        means = means + lax.dot_general(
            jnp.concatenate(left, axis=0),
            jnp.concatenate(right, axis=0),
            (((0,), (0,)), ((), ())),
            preferred_element_type=F32,
        )
        return sums[0], sums[1], means

    none = jnp.zeros((8, queries), F32)
    state = lax.fori_loop(
        0, steps, gather, (none, none, jnp.zeros((LANES, queries), F32)), unroll=2
    )
    lines, columns = [], []
    for kind in range(2):
        total = jnp.sum(state[kind], axis=0, keepdims=True)
        log = tops[kind] + jnp.log2(total)
        lines += [log[:, k : k + LANES] for k in range(0, queries, LANES)]
        mean = state[2][kind * HALF : kind * HALF + SH] * (1.0 / total)
        columns += [mean, jnp.broadcast_to(log, (HALF - SH, queries))]
    groups, own = out_ref.shape[0], out_ref.shape[1] - 8
    out_ref[:, :own, :] = jnp.concatenate(columns, axis=0).T.reshape(groups, own, LANES)
    out_ref[:, own:, :] = jnp.broadcast_to(
        jnp.concatenate(lines, axis=0)[None], (groups, 8, LANES)
    )


def grads_kernel(
    chunk, near_ref, logs_ref, weights_ref, own_ref, keys_ref, rows_ref, key_ref, own_out_ref,
    span_ref, mean_ref,
):
    deep = logs_ref.shape[1] - 8
    logs = logs_ref[:, deep:, :]
    high = jnp.max(logs, axis=0)
    logs = high + jnp.log2(jnp.sum(jnp.exp2(logs - high[None]), axis=0))
    lines = logs.shape[0] // 2
    flat = lambda rows: jnp.concatenate([rows[k : k + 1] for k in range(lines)], axis=1)
    teach_log, stud_log = flat(logs[:lines]), flat(logs[lines:])
    weights = weights_ref[...]
    teach_q, left_q, right_q = queries_of(near_ref, rows_ref)
    span_ref[0], span_ref[1], span_ref[2] = teach_q, left_q, right_q
    own = key_ref.shape[1]

    means = logs_ref[:, :deep, :]
    each = jnp.where(low_lanes(3), means[:, :, SH : SH + 1], means[:, :, HALF + SH : HALF + SH + 1])
    share = jnp.exp2(each - jnp.max(each, axis=0, keepdims=True))
    mean = jnp.sum(share * means, axis=0) / jnp.sum(share, axis=0)
    mean = (turn(mean) - mean) * own_ref[...] * (1.0 / math.sqrt(SH))
    mean_ref[...] = mean.reshape(mean_ref.shape)
    spot = near_ref[0] * CORES + near_ref[1]
    for step_to in range(NEAR * CORES):
        own_out_ref[step_to] = mean_ref[spot ^ step_to]

    def grad(teach_score, stud_score):
        teach = jnp.exp2(teach_score * (LOG2E / math.sqrt(TH)) - teach_log)
        stud = jnp.exp2(stud_score * (LOG2E / math.sqrt(SH)) - stud_log)
        return (weights * (stud - teach)).astype(BF16)

    def step(index, _):
        first, second, pack = key_chunk(keys_ref, index * chunk, chunk)
        left = grad(scores_of(span_ref[0], first), scores_of(span_ref[1], pack))
        right = grad(scores_of(span_ref[0], second), scores_of(span_ref[2], pack))
        mix = jnp.dot(left, span_ref[1], preferred_element_type=F32)
        mix = mix + jnp.dot(right, span_ref[2], preferred_element_type=F32)
        mix = (mix * (1.0 / math.sqrt(SH))).astype(key_ref.dtype)
        key_ref[pl.ds(index * chunk, chunk)] = mix.reshape(chunk, own, LANES)
        return 0

    lax.fori_loop(0, keys_ref.shape[0] // chunk, step, 0, unroll=2)


def unpack_keys(in_ref, out_ref):
    half = in_ref.shape[1]
    group = 16
    for start in range(0, in_ref.shape[0], group):
        for side in range(2):
            parts = [
                in_ref[head, :, side * HALF : side * HALF + SH].astype(F32)
                for head in range(start, start + group)
            ]
            out_ref[side * half : (side + 1) * half, start * SH : (start + group) * SH] = (
                jnp.concatenate(parts, axis=1)
            )


def unpack_rows(near_ref, mine_ref, along_ref, across_ref, out_ref, part_ref):
    spot = near_ref[0] * CORES + near_ref[1]
    part_ref[spot] = mine_ref[0]
    part_ref[spot ^ 2] = along_ref[0]
    part_ref[spot ^ 1] = across_ref[0]
    part_ref[spot ^ 3] = across_ref[1]
    out_ref[...] = jnp.concatenate(
        [part_ref[head, :, :SH] for head in range(part_ref.shape[0])], axis=1
    )


def call(body, shapes, scratch=(), smem=0, raw=0, raw_out=0, flops=0, room=48):
    kinds = [pltpu.SMEM, pltpu.HBM, pltpu.VMEM]
    specs = lambda counts: [
        pl.BlockSpec(memory_space=kind) for kind, count in zip(kinds, counts) for _ in range(count)
    ]

    def run(*args):
        many = isinstance(shapes, (list, tuple))
        outs = specs((0, raw_out, (len(shapes) if many else 1) - raw_out))
        moved = sum(arg.size * arg.dtype.itemsize for arg in args)
        return pl.pallas_call(
            body,
            out_shape=shapes,
            in_specs=specs((smem, raw, len(args) - smem - raw)),
            out_specs=outs if many else outs[0],
            scratch_shapes=list(scratch),
            cost_estimate=pl.CostEstimate(flops=flops, bytes_accessed=moved, transcendentals=0),
            compiler_params=pltpu.CompilerParams(vmem_limit_bytes=room * 2**20),
        )(*args)

    return run


def on_device(teacher_span, teacher_context, student_span, student_context, query_weights):
    groups, tps = lax.axis_size("group"), lax.axis_size("tp")
    heads = tps * NEAR * CORES
    near = NEAR * CORES
    rows_own, tokens_own = teacher_span.shape[0], teacher_context.shape[0]
    half = tokens_own // 2
    queries = query_weights.shape[0]
    shape = jax.ShapeDtypeStruct

    def trade(array, axes):
        return lax.all_to_all(array, axes, split_axis=0, concat_axis=0, tiled=True)

    core = lax.axis_index("core").astype(jnp.int32)
    spot = jnp.stack([lax.axis_index("near").astype(jnp.int32), core])
    piece = shape(((NEAR + 1) * rows_own, LANES), BF16)
    keys, kept, given = call(
        pack,
        (shape((heads, 3 * half, LANES), BF16), piece, piece),
        scratch=[
            pltpu.VMEM(teacher_span.shape, BF16),
            pltpu.VMEM(teacher_context.shape, BF16),
            pltpu.VMEM(student_span.shape, BF16),
            pltpu.VMEM(student_context.shape, BF16),
            pltpu.VMEM((heads, 3 * half, LANES), BF16),
            pltpu.SemaphoreType.DMA((8,)),
        ],
        smem=1,
        raw=4,
        raw_out=1,
        room=62,
    )(
        (spot[:1] ^ core),
        teacher_span,
        teacher_context,
        student_span,
        student_context,
    )
    other = lax.ppermute(given, "core", [(0, 1), (1, 0)])
    order = lambda first, second: jnp.stack(
        [part.reshape(NEAR + 1, rows_own, LANES) for part in (first, second)], axis=1
    )
    shard = jnp.where(core == 0, order(kept, other), order(other, kept))
    shard = shard.reshape(1, (NEAR + 1) * CORES * rows_own, LANES)
    keys = trade(keys, ("tp", "near", "core"))
    rows = lax.all_gather(
        shard,
        ("group", "near", "core"),
        axis=0,
        tiled=True,
        axis_index_groups=[
            [z * CORES + (z + side) % CORES for z in range(groups * NEAR)] for side in range(CORES)
        ],
    )

    spans = pltpu.VMEM((3, queries, LANES), BF16)
    deep = queries // groups
    logs = call(
        functools.partial(totals_kernel, 8),
        shape((groups, deep + 8, LANES), F32),
        scratch=[spans, pltpu.VMEM((4, heads * half, queries), F32)],
        smem=1,
        flops=2**31,
    )(spot, keys, rows)
    logs = trade(logs, "group")
    tokens_all = tokens_own * heads * groups
    weights = math.sqrt(tokens_all) * query_weights
    own = lax.dynamic_slice(weights, (lax.axis_index("group") * deep,), (deep,))
    own = jnp.broadcast_to(own[:, None], (deep, LANES))
    parts, mine = call(
        functools.partial(grads_kernel, 8),
        (shape((heads, half, LANES), BF16), shape((near, rows_own, LANES), F32)),
        scratch=[spans, pltpu.VMEM((near, rows_own, LANES), F32)],
        smem=1,
        flops=2**30,
    )(spot, logs, weights.reshape(1, queries), own, keys, rows)
    parts = trade(parts, ("tp", "near", "core"))
    flip = lambda array, axis: lax.ppermute(array, axis, [(0, 1), (1, 0)])
    along = flip(mine[CORES:], "near")
    across = flip(jnp.stack([mine[1], along[1]]), "core")
    grad_span = call(
        unpack_rows,
        shape((rows_own, near * SH), F32),
        scratch=[pltpu.VMEM((near, rows_own, LANES), F32)],
        smem=1,
    )(spot, mine, along, across)
    grad_context = call(unpack_keys, shape((tokens_own, heads * SH), F32))(parts)
    return (grad_span, grad_context)


def solution(mesh):
    ctx, tp = mesh.devices.shape
    split = Mesh(
        mesh.devices.reshape(ctx // (NEAR * CORES), NEAR, CORES, tp),
        ("group", "near", "core", "tp"),
    )
    rows = ("group", "near", "core")
    tokens = rows + ("tp",)
    placed = (P(rows, "tp"), P(tokens, None), P(rows, "tp"), P(tokens, None), P())
    return jax.shard_map(
        on_device,
        mesh=split,
        in_specs=placed,
        out_specs=(P(rows, "tp"), P(tokens, None)),
        check_vma=False,
    )
```

```python
import functools
import math

import jax
import jax.numpy as jnp
from jax import lax
from jax.experimental import pallas as pl
from jax.experimental.pallas import tpu as pltpu
from jax.sharding import Mesh, PartitionSpec as P

TH = 128
SH = 40
CORES = 2
NEAR = 2
LANES = 128
HALF = LANES // 2
LOG2E = math.log2(math.e)
F32 = jnp.float32
BF16 = jnp.bfloat16


def side_by_side(low, high):
    gap = jnp.zeros((low.shape[0], HALF - SH), low.dtype)
    return jnp.concatenate([low, gap, high, gap], axis=1)


def pack(side_ref, tq_hbm, tk_hbm, sq_hbm, sk_hbm, keys_hbm, kept_ref, given_ref,
         tq_ref, tk_ref, sq_ref, sk_ref, keys_ref, sems):
    heads, tokens, half = keys_hbm.shape[0], tk_hbm.shape[0], tk_hbm.shape[0] // 2
    fetches = [
        pltpu.make_async_copy(source, target, sems.at[number])
        for number, (source, target) in enumerate(
            [(tq_hbm, tq_ref), (sq_hbm, sq_ref), (sk_hbm, sk_ref), (tk_hbm, tk_ref)]
        )
    ]
    for copy in fetches:
        copy.start()
    rows = tq_ref.shape[0]

    def fill(out_ref, second):
        teach = [tq_ref[:, head * TH : (head + 1) * TH] for head in range(NEAR * CORES)]
        out_ref[:rows, :] = jnp.where(second, teach[1], teach[0])
        out_ref[rows : 2 * rows, :] = jnp.where(second, teach[2], teach[3])
        stud = [sq_ref[:, head * SH : (head + 1) * SH] for head in range(NEAR * CORES)]
        out_ref[2 * rows :, :] = jnp.where(
            second, side_by_side(stud[1], stud[2]), side_by_side(stud[0], stud[3])
        )

    fetches[0].wait()
    fetches[1].wait()
    second = side_ref[0] == 1
    fill(kept_ref, second)
    fill(given_ref, jnp.logical_not(second))
    fetches[2].wait()
    for head in range(heads):
        part = sk_ref[:, head * SH : (head + 1) * SH]
        keys_ref[head, tokens:, :] = side_by_side(part[:half], part[half:])
    fetches[3].wait()
    group = heads // 4
    sends = []
    for start in range(0, heads, group):
        for head in range(start, start + group):
            keys_ref[head, :tokens, :] = tk_ref[:, head * TH : (head + 1) * TH]
        here = pl.ds(start, group)
        sends.append(
            pltpu.make_async_copy(keys_ref.at[here], keys_hbm.at[here], sems.at[4 + start // group])
        )
        sends[-1].start()
    for copy in sends:
        copy.wait()


def queries_of(near_ref, rows_ref):
    count, deep, lanes = rows_ref.shape
    own = deep // (NEAR + 1)
    near = near_ref[0]
    start = pl.multiple_of(near * own, own)
    teach = rows_ref[:, pl.ds(start, own), :].reshape(count * own, lanes)
    stud = rows_ref[:, NEAR * own :, :].reshape(count * own, lanes).astype(F32)
    turned = jnp.concatenate([stud[:, HALF:], stud[:, :HALF]], axis=1)
    low = lax.broadcasted_iota(jnp.int32, (1, lanes), 1) < HALF
    first = near == 0
    left = jnp.where(low, jnp.where(first, stud, turned), 0.0)
    right = jnp.where(low, 0.0, jnp.where(first, turned, stud))
    return teach, left.astype(BF16), right.astype(BF16)


def key_chunk(keys_ref, start, size):
    part = keys_ref[pl.ds(start, size)]
    own = part.shape[1] // 3
    flat = lambda block: block.reshape(size * own, LANES)
    return flat(part[:, :own]), flat(part[:, own : 2 * own]), flat(part[:, 2 * own :])


def scores_of(span, key):
    return lax.dot_general(key, span, (((1,), (1,)), ((), ())), preferred_element_type=F32)


def turn(array):
    return jnp.concatenate([array[..., HALF:], array[..., :HALF]], axis=-1)


def low_lanes(rank):
    shape = (1,) * (rank - 1) + (LANES,)
    return lax.broadcasted_iota(jnp.int32, shape, rank - 1) < HALF


def totals_kernel(chunk, near_ref, keys_ref, rows_ref, out_ref, span_ref, score_ref):
    teach_q, left_q, right_q = queries_of(near_ref, rows_ref)
    span_ref[0], span_ref[1], span_ref[2] = teach_q, left_q, right_q
    queries = teach_q.shape[0]
    steps = keys_ref.shape[0] // chunk
    scales = (LOG2E / math.sqrt(TH), LOG2E / math.sqrt(SH))

    def measure(index, tops):
        first, second, pack = key_chunk(keys_ref, index * chunk, chunk)
        here = pl.ds(index * first.shape[0], first.shape[0])
        found = []
        for kind, span, key in ((0, 0, first), (0, 0, second), (1, 1, pack), (1, 2, pack)):
            score = scores_of(span_ref[span], key)
            score_ref[len(found), here] = score
            found.append(jnp.max(score.reshape(-1, 8, queries), axis=0))
        return jnp.maximum(tops[0], jnp.maximum(found[0], found[1])), jnp.maximum(
            tops[1], jnp.maximum(found[2], found[3])
        )

    start = jnp.full((8, queries), -1e30, F32)
    tops = lax.fori_loop(0, steps, measure, (start, start), unroll=True)
    tops = [jnp.max(top, axis=0, keepdims=True) * scale for top, scale in zip(tops, scales)]

    def gather(index, state):
        sums, means = list(state[:2]), state[2]
        _, _, pack = key_chunk(keys_ref, index * chunk, chunk)
        here = pl.ds(index * pack.shape[0], pack.shape[0])
        low = low_lanes(2)
        none = jnp.zeros_like(pack)
        turned = turn(pack.astype(F32)).astype(BF16)
        keys = (
            jnp.where(low, pack, none),
            jnp.where(low, turned, none),
            jnp.where(low, none, turned),
            jnp.where(low, none, pack),
        )
        left, right = [], []
        for number in range(4):
            kind = number // 2
            prob = jnp.exp2(score_ref[number, here] * scales[kind] - tops[kind])
            sums[kind] = sums[kind] + jnp.sum(prob.reshape(-1, 8, queries), axis=0)
            high = prob.astype(BF16)
            left += [keys[number], keys[number]]
            right += [high, (prob - high.astype(F32)).astype(BF16)]
        means = means + lax.dot_general(
            jnp.concatenate(left, axis=0),
            jnp.concatenate(right, axis=0),
            (((0,), (0,)), ((), ())),
            preferred_element_type=F32,
        )
        return sums[0], sums[1], means

    none = jnp.zeros((8, queries), F32)
    state = lax.fori_loop(
        0, steps, gather, (none, none, jnp.zeros((LANES, queries), F32)), unroll=True
    )
    lines, columns = [], []
    for kind in range(2):
        total = jnp.sum(state[kind], axis=0, keepdims=True)
        log = tops[kind] + jnp.log2(total)
        lines += [log[:, k : k + LANES] for k in range(0, queries, LANES)]
        mean = state[2][kind * HALF : kind * HALF + SH] * (1.0 / total)
        columns += [mean, jnp.broadcast_to(log, (HALF - SH, queries))]
    groups, own = out_ref.shape[0], out_ref.shape[1] - 8
    out_ref[:, :own, :] = jnp.concatenate(columns, axis=0).T.reshape(groups, own, LANES)
    out_ref[:, own:, :] = jnp.broadcast_to(
        jnp.concatenate(lines, axis=0)[None], (groups, 8, LANES)
    )


def grads_kernel(
    chunk, near_ref, core_ref, logs_ref, weights_ref, own_ref, keys_ref, span_ref, key_ref,
    own_out_ref, mean_ref,
):
    deep = logs_ref.shape[1] - 8
    logs = logs_ref[:, deep:, :]
    high = jnp.max(logs, axis=0)
    logs = high + jnp.log2(jnp.sum(jnp.exp2(logs - high[None]), axis=0))
    lines = logs.shape[0] // 2
    flat = lambda rows: jnp.concatenate([rows[k : k + 1] for k in range(lines)], axis=1)
    teach_log, stud_log = flat(logs[:lines]), flat(logs[lines:])
    weights = weights_ref[...]
    own = key_ref.shape[1]

    means = logs_ref[:, :deep, :]
    each = jnp.where(low_lanes(3), means[:, :, SH : SH + 1], means[:, :, HALF + SH : HALF + SH + 1])
    share = jnp.exp2(each - jnp.max(each, axis=0, keepdims=True))
    mean = jnp.sum(share * means, axis=0) / jnp.sum(share, axis=0)
    mean = (turn(mean) - mean) * own_ref[...] * (1.0 / math.sqrt(SH))
    mean_ref[...] = mean.reshape(mean_ref.shape)
    spot = near_ref[0] * CORES + core_ref[0]
    for step_to in range(NEAR * CORES):
        own_out_ref[step_to] = mean_ref[spot ^ step_to]

    def grad(teach_score, stud_score):
        teach = jnp.exp2(teach_score * (LOG2E / math.sqrt(TH)) - teach_log)
        stud = jnp.exp2(stud_score * (LOG2E / math.sqrt(SH)) - stud_log)
        return (weights * (stud - teach)).astype(BF16)

    def step(index, _):
        first, second, pack = key_chunk(keys_ref, index * chunk, chunk)
        left = grad(scores_of(span_ref[0], first), scores_of(span_ref[1], pack))
        right = grad(scores_of(span_ref[0], second), scores_of(span_ref[2], pack))
        mix = jnp.dot(left, span_ref[1], preferred_element_type=F32)
        mix = mix + jnp.dot(right, span_ref[2], preferred_element_type=F32)
        mix = (mix * (1.0 / math.sqrt(SH))).astype(key_ref.dtype)
        key_ref[pl.ds(index * chunk, chunk)] = mix.reshape(chunk, own, LANES)
        return 0

    lax.fori_loop(0, keys_ref.shape[0] // chunk, step, 0, unroll=True)


def unpack_keys(in_ref, out_ref):
    half = in_ref.shape[1]
    group = 16
    for start in range(0, in_ref.shape[0], group):
        for side in range(2):
            parts = [
                in_ref[head, :, side * HALF : side * HALF + SH].astype(F32)
                for head in range(start, start + group)
            ]
            out_ref[side * half : (side + 1) * half, start * SH : (start + group) * SH] = (
                jnp.concatenate(parts, axis=1)
            )


def unpack_rows(near_ref, core_ref, mine_ref, along_ref, across_ref, out_ref, part_ref):
    spot = near_ref[0] * CORES + core_ref[0]
    part_ref[spot] = mine_ref[0]
    part_ref[spot ^ 2] = along_ref[0]
    part_ref[spot ^ 1] = across_ref[0]
    part_ref[spot ^ 3] = across_ref[1]
    out_ref[...] = jnp.concatenate(
        [part_ref[head, :, :SH] for head in range(part_ref.shape[0])], axis=1
    )


def call(body, shapes, scratch=(), smem=0, raw=0, raw_out=0, flops=0, room=48):
    kinds = [pltpu.SMEM, pltpu.HBM, pltpu.VMEM]
    specs = lambda counts: [
        pl.BlockSpec(memory_space=kind) for kind, count in zip(kinds, counts) for _ in range(count)
    ]

    def run(*args):
        many = isinstance(shapes, (list, tuple))
        outs = specs((0, raw_out, (len(shapes) if many else 1) - raw_out))
        moved = sum(arg.size * arg.dtype.itemsize for arg in args)
        return pl.pallas_call(
            body,
            out_shape=shapes,
            in_specs=specs((smem, raw, len(args) - smem - raw)),
            out_specs=outs if many else outs[0],
            scratch_shapes=list(scratch),
            cost_estimate=pl.CostEstimate(flops=flops, bytes_accessed=moved, transcendentals=0),
            compiler_params=pltpu.CompilerParams(vmem_limit_bytes=room * 2**20),
        )(*args)

    return run


def on_device(teacher_span, teacher_context, student_span, student_context, query_weights):
    groups, tps = lax.axis_size("group"), lax.axis_size("tp")
    heads = tps * NEAR * CORES
    near = NEAR * CORES
    rows_own, tokens_own = teacher_span.shape[0], teacher_context.shape[0]
    half = tokens_own // 2
    queries = query_weights.shape[0]
    shape = jax.ShapeDtypeStruct

    def trade(array, axes):
        return lax.all_to_all(array, axes, split_axis=0, concat_axis=0, tiled=True)

    core = lax.axis_index("core").astype(jnp.int32)
    side = core.reshape(1)
    spot = lax.axis_index("near").astype(jnp.int32).reshape(1)
    piece = shape(((NEAR + 1) * rows_own, LANES), BF16)
    keys, kept, given = call(
        pack,
        (shape((heads, 3 * half, LANES), BF16), piece, piece),
        scratch=[
            pltpu.VMEM(teacher_span.shape, BF16),
            pltpu.VMEM(teacher_context.shape, BF16),
            pltpu.VMEM(student_span.shape, BF16),
            pltpu.VMEM(student_context.shape, BF16),
            pltpu.VMEM((heads, 3 * half, LANES), BF16),
            pltpu.SemaphoreType.DMA((8,)),
        ],
        smem=1,
        raw=4,
        raw_out=1,
        room=62,
    )(
        spot ^ side,
        teacher_span,
        teacher_context,
        student_span,
        student_context,
    )
    other = lax.ppermute(given, "core", [(0, 1), (1, 0)])
    order = lambda first, second: jnp.stack(
        [part.reshape(NEAR + 1, rows_own, LANES) for part in (first, second)], axis=1
    )
    shard = jnp.where(core == 0, order(kept, other), order(other, kept))
    shard = shard.reshape(1, (NEAR + 1) * CORES * rows_own, LANES)
    keys = trade(keys, ("tp", "near", "core"))
    rows = lax.all_gather(
        shard,
        ("group", "near", "core"),
        axis=0,
        tiled=True,
        axis_index_groups=[
            [z * CORES + (z + side) % CORES for z in range(groups * NEAR)] for side in range(CORES)
        ],
    )

    deep = queries // groups
    logs, spans = call(
        functools.partial(totals_kernel, 8),
        (shape((groups, deep + 8, LANES), F32), shape((3, queries, LANES), BF16)),
        scratch=[pltpu.VMEM((4, heads * half, queries), F32)],
        smem=1,
        flops=2**31,
    )(spot, keys, rows)
    logs = trade(logs, "group")
    tokens_all = tokens_own * heads * groups
    weights = math.sqrt(tokens_all) * query_weights
    own = lax.dynamic_slice(weights, (lax.axis_index("group") * deep,), (deep,))
    own = jnp.broadcast_to(own[:, None], (deep, LANES))
    parts, mine = call(
        functools.partial(grads_kernel, 8),
        (shape((heads, half, LANES), BF16), shape((near, rows_own, LANES), F32)),
        scratch=[pltpu.VMEM((near, rows_own, LANES), F32)],
        smem=2,
        flops=2**30,
    )(spot, side, logs, weights.reshape(1, queries), own, keys, spans)
    parts = trade(parts, ("tp", "near", "core"))
    flip = lambda array, axis: lax.ppermute(array, axis, [(0, 1), (1, 0)])
    along = flip(mine[CORES:], "near")
    across = flip(jnp.stack([mine[1], along[1]]), "core")
    grad_span = call(
        unpack_rows,
        shape((rows_own, near * SH), F32),
        scratch=[pltpu.VMEM((near, rows_own, LANES), F32)],
        smem=2,
    )(spot, side, mine, along, across)
    grad_context = call(unpack_keys, shape((tokens_own, heads * SH), F32))(parts)
    return (grad_span, grad_context)


def solution(mesh):
    ctx, tp = mesh.devices.shape
    split = Mesh(
        mesh.devices.reshape(ctx // (NEAR * CORES), NEAR, CORES, tp),
        ("group", "near", "core", "tp"),
    )
    rows = ("group", "near", "core")
    tokens = rows + ("tp",)
    placed = (P(rows, "tp"), P(tokens, None), P(rows, "tp"), P(tokens, None), P())
    return jax.shard_map(
        on_device,
        mesh=split,
        in_specs=placed,
        out_specs=(P(rows, "tp"), P(tokens, None)),
        check_vma=False,
    )
```

```python
import functools
import math

import jax
import jax.numpy as jnp
from jax import lax
from jax.experimental import pallas as pl
from jax.experimental.pallas import tpu as pltpu
from jax.sharding import Mesh, PartitionSpec as P

TH = 128
SH = 40
CORES = 2
NEAR = 2
LANES = 128
HALF = LANES // 2
LOG2E = math.log2(math.e)
F32 = jnp.float32
BF16 = jnp.bfloat16


def side_by_side(low, high):
    gap = jnp.zeros((low.shape[0], HALF - SH), low.dtype)
    return jnp.concatenate([low, gap, high, gap], axis=1)


def pack(side_ref, tq_hbm, tk_hbm, sq_hbm, sk_hbm, keys_hbm, kept_ref, given_ref,
         tq_ref, tk_ref, sq_ref, sk_ref, keys_ref, sems):
    heads, tokens, half = keys_hbm.shape[0], tk_hbm.shape[0], tk_hbm.shape[0] // 2
    fetches = [
        pltpu.make_async_copy(source, target, sems.at[number])
        for number, (source, target) in enumerate(
            [(tq_hbm, tq_ref), (sq_hbm, sq_ref), (sk_hbm, sk_ref), (tk_hbm, tk_ref)]
        )
    ]
    for copy in fetches:
        copy.start()
    rows = tq_ref.shape[0]

    def fill(out_ref, second):
        teach = [tq_ref[:, head * TH : (head + 1) * TH] for head in range(NEAR * CORES)]
        out_ref[:rows, :] = jnp.where(second, teach[1], teach[0])
        out_ref[rows : 2 * rows, :] = jnp.where(second, teach[2], teach[3])
        stud = [sq_ref[:, head * SH : (head + 1) * SH] for head in range(NEAR * CORES)]
        out_ref[2 * rows :, :] = jnp.where(
            second, side_by_side(stud[1], stud[2]), side_by_side(stud[0], stud[3])
        )

    fetches[0].wait()
    fetches[1].wait()
    second = side_ref[0] == 1
    fill(kept_ref, second)
    fill(given_ref, jnp.logical_not(second))
    fetches[2].wait()
    for head in range(heads):
        part = sk_ref[:, head * SH : (head + 1) * SH]
        keys_ref[head, tokens:, :] = side_by_side(part[:half], part[half:])
    fetches[3].wait()
    group = heads // 4
    sends = []
    for start in range(0, heads, group):
        for head in range(start, start + group):
            keys_ref[head, :tokens, :] = tk_ref[:, head * TH : (head + 1) * TH]
        here = pl.ds(start, group)
        sends.append(
            pltpu.make_async_copy(keys_ref.at[here], keys_hbm.at[here], sems.at[4 + start // group])
        )
        sends[-1].start()
    for copy in sends:
        copy.wait()


def queries_of(near_ref, rows_ref):
    count, deep, lanes = rows_ref.shape
    own = deep // (NEAR + 1)
    near = near_ref[0]
    start = pl.multiple_of(near * own, own)
    teach = rows_ref[:, pl.ds(start, own), :].reshape(count * own, lanes)
    stud = rows_ref[:, NEAR * own :, :].reshape(count * own, lanes).astype(F32)
    turned = jnp.concatenate([stud[:, HALF:], stud[:, :HALF]], axis=1)
    low = lax.broadcasted_iota(jnp.int32, (1, lanes), 1) < HALF
    first = near == 0
    left = jnp.where(low, jnp.where(first, stud, turned), 0.0)
    right = jnp.where(low, 0.0, jnp.where(first, turned, stud))
    return teach, left.astype(BF16), right.astype(BF16)


def key_chunk(keys_ref, start, size):
    part = keys_ref[pl.ds(start, size)]
    own = part.shape[1] // 3
    flat = lambda block: block.reshape(size * own, LANES)
    return flat(part[:, :own]), flat(part[:, own : 2 * own]), flat(part[:, 2 * own :])


def scores_of(span, key):
    return lax.dot_general(key, span, (((1,), (1,)), ((), ())), preferred_element_type=F32)


def turn(array):
    return jnp.concatenate([array[..., HALF:], array[..., :HALF]], axis=-1)


def low_lanes(rank):
    shape = (1,) * (rank - 1) + (LANES,)
    return lax.broadcasted_iota(jnp.int32, shape, rank - 1) < HALF


UNIT = SH + 2


def squeeze(means):
    teach, stud = means[:, :, :UNIT], means[:, :, HALF : HALF + UNIT]
    rows = means.shape[1]
    deep = 3 * rows // 4
    rest = rows - (deep - (rows - deep))
    none = jnp.zeros_like(stud[:, : deep - rest])
    second = jnp.concatenate([teach[:, deep:], stud[:, : rows - rest]], axis=1)
    third = jnp.concatenate([stud[:, rows - rest :], none], axis=1)
    gap = jnp.zeros(third.shape[:2] + (LANES - 3 * UNIT,), F32)
    return jnp.concatenate([teach[:, :deep], second, third, gap], axis=2)


def spread(packed):
    deep = packed.shape[1]
    rows = deep * 4 // 3
    rest = rows - (deep - (rows - deep))
    first, second, third = (packed[:, :, k * UNIT : (k + 1) * UNIT] for k in range(3))
    teach = jnp.concatenate([first, second[:, : rows - deep]], axis=1)
    stud = jnp.concatenate([second[:, rows - deep :], third[:, :rest]], axis=1)
    return teach, stud


def totals_kernel(chunk, wide, near_ref, keys_ref, rows_ref, out_ref, span_ref, score_ref):
    teach_q, left_q, right_q = queries_of(near_ref, rows_ref)
    span_ref[0], span_ref[1], span_ref[2] = teach_q, left_q, right_q
    queries = teach_q.shape[0]
    steps = keys_ref.shape[0] // chunk
    scales = (LOG2E / math.sqrt(TH), LOG2E / math.sqrt(SH))

    def measure(index, tops):
        first, second, pack = key_chunk(keys_ref, index * wide, wide)
        here = pl.ds(index * first.shape[0], first.shape[0])
        found = []
        for kind, span, key in ((0, 0, first), (0, 0, second), (1, 1, pack), (1, 2, pack)):
            score = scores_of(span_ref[span], key)
            score_ref[len(found), here] = score
            found.append(jnp.max(score.reshape(-1, 8, queries), axis=0))
        return jnp.maximum(tops[0], jnp.maximum(found[0], found[1])), jnp.maximum(
            tops[1], jnp.maximum(found[2], found[3])
        )

    start = jnp.full((8, queries), -1e30, F32)
    tops = lax.fori_loop(0, keys_ref.shape[0] // wide, measure, (start, start), unroll=True)
    tops = [jnp.max(top, axis=0, keepdims=True) * scale for top, scale in zip(tops, scales)]

    def gather(index, state):
        sums, means = list(state[:2]), state[2]
        _, _, pack = key_chunk(keys_ref, index * chunk, chunk)
        here = pl.ds(index * pack.shape[0], pack.shape[0])
        low = low_lanes(2)
        none = jnp.zeros_like(pack)
        turned = turn(pack.astype(F32)).astype(BF16)
        keys = (
            jnp.where(low, pack, none),
            jnp.where(low, turned, none),
            jnp.where(low, none, turned),
            jnp.where(low, none, pack),
        )
        left, right = [], []
        for number in range(4):
            kind = number // 2
            prob = jnp.exp2(score_ref[number, here] * scales[kind] - tops[kind])
            sums[kind] = sums[kind] + jnp.sum(prob.reshape(-1, 8, queries), axis=0)
            high = prob.astype(BF16)
            left += [keys[number], keys[number]]
            right += [high, (prob - high.astype(F32)).astype(BF16)]
        means = means + lax.dot_general(
            jnp.concatenate(left, axis=0),
            jnp.concatenate(right, axis=0),
            (((0,), (0,)), ((), ())),
            preferred_element_type=F32,
        )
        return sums[0], sums[1], means

    none = jnp.zeros((8, queries), F32)
    state = lax.fori_loop(
        0, steps, gather, (none, none, jnp.zeros((LANES, queries), F32)), unroll=True
    )
    lines, columns = [], []
    for kind in range(2):
        total = jnp.sum(state[kind], axis=0, keepdims=True)
        log = tops[kind] + jnp.log2(total)
        lines += [log[:, k : k + LANES] for k in range(0, queries, LANES)]
        mean = state[2][kind * HALF : kind * HALF + SH] * (1.0 / total)
        columns += [mean, jnp.broadcast_to(log, (HALF - SH, queries))]
    groups, own = out_ref.shape[0], out_ref.shape[1] - 8
    means = jnp.concatenate(columns, axis=0).T.reshape(groups, queries // groups, LANES)
    out_ref[:, :own, :] = squeeze(means)
    out_ref[:, own:, :] = jnp.broadcast_to(
        jnp.concatenate(lines, axis=0)[None], (groups, 8, LANES)
    )


def grads_kernel(
    chunk, near_ref, core_ref, logs_ref, weights_ref, own_ref, keys_ref, span_ref, key_ref,
    own_out_ref, mean_ref,
):
    deep = logs_ref.shape[1] - 8
    logs = logs_ref[:, deep:, :]
    high = jnp.max(logs, axis=0)
    logs = high + jnp.log2(jnp.sum(jnp.exp2(logs - high[None]), axis=0))
    lines = logs.shape[0] // 2
    flat = lambda rows: jnp.concatenate([rows[k : k + 1] for k in range(lines)], axis=1)
    teach_log, stud_log = flat(logs[:lines]), flat(logs[lines:])
    weights = weights_ref[...]
    own = key_ref.shape[1]

    found = []
    for part in spread(logs_ref[:, :deep, :]):
        each = part[:, :, SH : SH + 1]
        share = jnp.exp2(each - jnp.max(each, axis=0, keepdims=True))
        found.append(jnp.sum(share * part, axis=0) / jnp.sum(share, axis=0))
    mean = (found[1] - found[0]) * own_ref[:, :UNIT] * (1.0 / math.sqrt(SH))
    mean = jnp.concatenate([mean, jnp.zeros((mean.shape[0], LANES - UNIT), F32)], axis=1)
    mean_ref[...] = mean.reshape(mean_ref.shape)
    spot = near_ref[0] * CORES + core_ref[0]
    for step_to in range(NEAR * CORES):
        own_out_ref[step_to] = mean_ref[spot ^ step_to]

    def grad(teach_score, stud_score):
        teach = jnp.exp2(teach_score * (LOG2E / math.sqrt(TH)) - teach_log)
        stud = jnp.exp2(stud_score * (LOG2E / math.sqrt(SH)) - stud_log)
        return (weights * (stud - teach)).astype(BF16)

    def step(index, _):
        first, second, pack = key_chunk(keys_ref, index * chunk, chunk)
        left = grad(scores_of(span_ref[0], first), scores_of(span_ref[1], pack))
        right = grad(scores_of(span_ref[0], second), scores_of(span_ref[2], pack))
        mix = jnp.dot(left, span_ref[1], preferred_element_type=F32)
        mix = mix + jnp.dot(right, span_ref[2], preferred_element_type=F32)
        mix = (mix * (1.0 / math.sqrt(SH))).astype(key_ref.dtype)
        key_ref[pl.ds(index * chunk, chunk)] = mix.reshape(chunk, own, LANES)
        return 0

    lax.fori_loop(0, keys_ref.shape[0] // chunk, step, 0, unroll=True)


def unpack_keys(in_ref, out_ref):
    half = in_ref.shape[1]
    group = 16
    for start in range(0, in_ref.shape[0], group):
        for side in range(2):
            parts = [
                in_ref[head, :, side * HALF : side * HALF + SH].astype(F32)
                for head in range(start, start + group)
            ]
            out_ref[side * half : (side + 1) * half, start * SH : (start + group) * SH] = (
                jnp.concatenate(parts, axis=1)
            )


def unpack_rows(near_ref, core_ref, mine_ref, along_ref, across_ref, out_ref, part_ref):
    spot = near_ref[0] * CORES + core_ref[0]
    part_ref[spot] = mine_ref[0]
    part_ref[spot ^ 2] = along_ref[0]
    part_ref[spot ^ 1] = across_ref[0]
    part_ref[spot ^ 3] = across_ref[1]
    out_ref[...] = jnp.concatenate(
        [part_ref[head, :, :SH] for head in range(part_ref.shape[0])], axis=1
    )


def call(body, shapes, scratch=(), smem=0, raw=0, raw_out=0, flops=0, room=48):
    kinds = [pltpu.SMEM, pltpu.HBM, pltpu.VMEM]
    specs = lambda counts: [
        pl.BlockSpec(memory_space=kind) for kind, count in zip(kinds, counts) for _ in range(count)
    ]

    def run(*args):
        many = isinstance(shapes, (list, tuple))
        outs = specs((0, raw_out, (len(shapes) if many else 1) - raw_out))
        moved = sum(arg.size * arg.dtype.itemsize for arg in args)
        return pl.pallas_call(
            body,
            out_shape=shapes,
            in_specs=specs((smem, raw, len(args) - smem - raw)),
            out_specs=outs if many else outs[0],
            scratch_shapes=list(scratch),
            cost_estimate=pl.CostEstimate(flops=flops, bytes_accessed=moved, transcendentals=0),
            compiler_params=pltpu.CompilerParams(vmem_limit_bytes=room * 2**20),
        )(*args)

    return run


def on_device(teacher_span, teacher_context, student_span, student_context, query_weights):
    groups, tps = lax.axis_size("group"), lax.axis_size("tp")
    heads = tps * NEAR * CORES
    near = NEAR * CORES
    rows_own, tokens_own = teacher_span.shape[0], teacher_context.shape[0]
    half = tokens_own // 2
    queries = query_weights.shape[0]
    shape = jax.ShapeDtypeStruct

    def trade(array, axes):
        return lax.all_to_all(array, axes, split_axis=0, concat_axis=0, tiled=True)

    core = lax.axis_index("core").astype(jnp.int32)
    side = core.reshape(1)
    spot = lax.axis_index("near").astype(jnp.int32).reshape(1)
    piece = shape(((NEAR + 1) * rows_own, LANES), BF16)
    keys, kept, given = call(
        pack,
        (shape((heads, 3 * half, LANES), BF16), piece, piece),
        scratch=[
            pltpu.VMEM(teacher_span.shape, BF16),
            pltpu.VMEM(teacher_context.shape, BF16),
            pltpu.VMEM(student_span.shape, BF16),
            pltpu.VMEM(student_context.shape, BF16),
            pltpu.VMEM((heads, 3 * half, LANES), BF16),
            pltpu.SemaphoreType.DMA((8,)),
        ],
        smem=1,
        raw=4,
        raw_out=1,
        room=62,
    )(
        spot ^ side,
        teacher_span,
        teacher_context,
        student_span,
        student_context,
    )
    other = lax.ppermute(given, "core", [(0, 1), (1, 0)])
    order = lambda first, second: jnp.stack(
        [part.reshape(NEAR + 1, rows_own, LANES) for part in (first, second)], axis=1
    )
    shard = jnp.where(core == 0, order(kept, other), order(other, kept))
    shard = shard.reshape(1, (NEAR + 1) * CORES * rows_own, LANES)
    keys = trade(keys, ("tp", "near", "core"))
    rows = lax.all_gather(
        shard,
        ("group", "near", "core"),
        axis=0,
        tiled=True,
        axis_index_groups=[
            [z * CORES + (z + side) % CORES for z in range(groups * NEAR)] for side in range(CORES)
        ],
    )

    deep = queries // groups
    logs, spans = call(
        functools.partial(totals_kernel, 8, 32),
        (shape((groups, 3 * deep // 4 + 8, LANES), F32), shape((3, queries, LANES), BF16)),
        scratch=[pltpu.VMEM((4, heads * half, queries), F32)],
        smem=1,
        flops=2**31,
    )(spot, keys, rows)
    logs = trade(logs, "group")
    tokens_all = tokens_own * heads * groups
    weights = math.sqrt(tokens_all) * query_weights
    own = lax.dynamic_slice(weights, (lax.axis_index("group") * deep,), (deep,))
    own = jnp.broadcast_to(own[:, None], (deep, LANES))
    parts, mine = call(
        functools.partial(grads_kernel, 8),
        (shape((heads, half, LANES), BF16), shape((near, rows_own, LANES), F32)),
        scratch=[pltpu.VMEM((near, rows_own, LANES), F32)],
        smem=2,
        flops=2**30,
    )(spot, side, logs, weights.reshape(1, queries), own, keys, spans)
    parts = trade(parts, ("tp", "near", "core"))
    flip = lambda array, axis: lax.ppermute(array, axis, [(0, 1), (1, 0)])
    along = flip(mine[CORES:], "near")
    across = flip(jnp.stack([mine[1], along[1]]), "core")
    grad_span = call(
        unpack_rows,
        shape((rows_own, near * SH), F32),
        scratch=[pltpu.VMEM((near, rows_own, LANES), F32)],
        smem=2,
    )(spot, side, mine, along, across)
    grad_context = call(unpack_keys, shape((tokens_own, heads * SH), F32))(parts)
    return (grad_span, grad_context)


def solution(mesh):
    ctx, tp = mesh.devices.shape
    split = Mesh(
        mesh.devices.reshape(ctx // (NEAR * CORES), NEAR, CORES, tp),
        ("group", "near", "core", "tp"),
    )
    rows = ("group", "near", "core")
    tokens = rows + ("tp",)
    placed = (P(rows, "tp"), P(tokens, None), P(rows, "tp"), P(tokens, None), P())
    return jax.shard_map(
        on_device,
        mesh=split,
        in_specs=placed,
        out_specs=(P(rows, "tp"), P(tokens, None)),
        check_vma=False,
    )
```

```python
import functools
import math

import jax
import jax.numpy as jnp
from jax import lax
from jax.experimental import pallas as pl
from jax.experimental.pallas import tpu as pltpu
from jax.sharding import Mesh, PartitionSpec as P

TH = 128
SH = 40
CORES = 2
NEAR = 2
LANES = 128
HALF = LANES // 2
LOG2E = math.log2(math.e)
F32 = jnp.float32
BF16 = jnp.bfloat16


def side_by_side(low, high):
    gap = jnp.zeros((low.shape[0], HALF - SH), low.dtype)
    return jnp.concatenate([low, gap, high, gap], axis=1)


def pack(side_ref, turn_ref, tq_hbm, tk_hbm, sq_hbm, sk_hbm, keys_hbm, kept_ref, given_ref,
         tq_ref, tk_ref, sq_ref, sk_ref, keys_ref, sems):
    heads, tokens, half = keys_hbm.shape[0], tk_hbm.shape[0], tk_hbm.shape[0] // 2
    fetches = [
        pltpu.make_async_copy(source, target, sems.at[number])
        for number, (source, target) in enumerate(
            [(tq_hbm, tq_ref), (sq_hbm, sq_ref), (sk_hbm, sk_ref), (tk_hbm, tk_ref)]
        )
    ]
    for copy in fetches:
        copy.start()
    rows = tq_ref.shape[0]

    def fill(out_ref, second):
        teach = [tq_ref[:, head * TH : (head + 1) * TH] for head in range(NEAR * CORES)]
        out_ref[:rows, :] = jnp.where(second, teach[1], teach[0])
        out_ref[rows : 2 * rows, :] = jnp.where(second, teach[2], teach[3])
        stud = [sq_ref[:, head * SH : (head + 1) * SH] for head in range(NEAR * CORES)]
        out_ref[2 * rows :, :] = jnp.where(
            second, side_by_side(stud[1], stud[2]), side_by_side(stud[0], stud[3])
        )

    fetches[0].wait()
    fetches[1].wait()
    second = side_ref[0] == 1
    fill(kept_ref, second)
    fill(given_ref, jnp.logical_not(second))
    fetches[2].wait()
    for head in range(heads):
        part = sk_ref[:, head * SH : (head + 1) * SH]
        keys_ref[head ^ turn_ref[0], tokens:, :] = side_by_side(part[:half], part[half:])
    fetches[3].wait()
    group = heads // 4
    sends = []
    for start in range(0, heads, group):
        for head in range(start, start + group):
            keys_ref[head ^ turn_ref[0], :tokens, :] = tk_ref[:, head * TH : (head + 1) * TH]
        here = pl.ds(start, group)
        sends.append(
            pltpu.make_async_copy(keys_ref.at[here], keys_hbm.at[here], sems.at[4 + start // group])
        )
        sends[-1].start()
    for copy in sends:
        copy.wait()


def queries_of(near_ref, rows_ref):
    count, deep, lanes = rows_ref.shape
    own = deep // (NEAR + 1)
    near = near_ref[0]
    start = pl.multiple_of(near * own, own)
    teach = rows_ref[:, pl.ds(start, own), :].reshape(count * own, lanes)
    stud = rows_ref[:, NEAR * own :, :].reshape(count * own, lanes).astype(F32)
    turned = jnp.concatenate([stud[:, HALF:], stud[:, :HALF]], axis=1)
    low = lax.broadcasted_iota(jnp.int32, (1, lanes), 1) < HALF
    first = near == 0
    left = jnp.where(low, jnp.where(first, stud, turned), 0.0)
    right = jnp.where(low, 0.0, jnp.where(first, turned, stud))
    return teach, left.astype(BF16), right.astype(BF16)


def key_chunk(keys_ref, start, size):
    part = keys_ref[pl.ds(start, size)]
    own = part.shape[1] // 3
    flat = lambda block: block.reshape(size * own, LANES)
    return flat(part[:, :own]), flat(part[:, own : 2 * own]), flat(part[:, 2 * own :])


def scores_of(span, key):
    return lax.dot_general(key, span, (((1,), (1,)), ((), ())), preferred_element_type=F32)


def turn(array):
    return jnp.concatenate([array[..., HALF:], array[..., :HALF]], axis=-1)


def low_lanes(rank):
    shape = (1,) * (rank - 1) + (LANES,)
    return lax.broadcasted_iota(jnp.int32, shape, rank - 1) < HALF


UNIT = SH + 2


def squeeze(means):
    teach, stud = means[:, :, :UNIT], means[:, :, HALF : HALF + UNIT]
    rows = means.shape[1]
    deep = 3 * rows // 4
    rest = rows - (deep - (rows - deep))
    none = jnp.zeros_like(stud[:, : deep - rest])
    second = jnp.concatenate([teach[:, deep:], stud[:, : rows - rest]], axis=1)
    third = jnp.concatenate([stud[:, rows - rest :], none], axis=1)
    gap = jnp.zeros(third.shape[:2] + (LANES - 3 * UNIT,), F32)
    return jnp.concatenate([teach[:, :deep], second, third, gap], axis=2)


def spread(packed):
    deep = packed.shape[1]
    rows = deep * 4 // 3
    rest = rows - (deep - (rows - deep))
    first, second, third = (packed[:, :, k * UNIT : (k + 1) * UNIT] for k in range(3))
    teach = jnp.concatenate([first, second[:, : rows - deep]], axis=1)
    stud = jnp.concatenate([second[:, rows - deep :], third[:, :rest]], axis=1)
    return teach, stud


def totals_kernel(chunk, wide, near_ref, keys_ref, rows_ref, out_ref, span_ref, score_ref):
    teach_q, left_q, right_q = queries_of(near_ref, rows_ref)
    span_ref[0], span_ref[1], span_ref[2] = teach_q, left_q, right_q
    queries = teach_q.shape[0]
    steps = keys_ref.shape[0] // chunk
    scales = (LOG2E / math.sqrt(TH), LOG2E / math.sqrt(SH))

    def measure(index, tops):
        first, second, pack = key_chunk(keys_ref, index * wide, wide)
        here = pl.ds(index * first.shape[0], first.shape[0])
        found = []
        for kind, span, key in ((0, 0, first), (0, 0, second), (1, 1, pack), (1, 2, pack)):
            score = scores_of(span_ref[span], key)
            score_ref[len(found), here] = score
            found.append(jnp.max(score.reshape(-1, 8, queries), axis=0))
        return jnp.maximum(tops[0], jnp.maximum(found[0], found[1])), jnp.maximum(
            tops[1], jnp.maximum(found[2], found[3])
        )

    start = jnp.full((8, queries), -1e30, F32)
    tops = lax.fori_loop(0, keys_ref.shape[0] // wide, measure, (start, start), unroll=True)
    tops = [jnp.max(top, axis=0, keepdims=True) * scale for top, scale in zip(tops, scales)]

    def gather(index, state):
        sums, means = list(state[:2]), state[2]
        _, _, pack = key_chunk(keys_ref, index * chunk, chunk)
        here = pl.ds(index * pack.shape[0], pack.shape[0])
        low = low_lanes(2)
        none = jnp.zeros_like(pack)
        turned = turn(pack.astype(F32)).astype(BF16)
        keys = (
            jnp.where(low, pack, none),
            jnp.where(low, turned, none),
            jnp.where(low, none, turned),
            jnp.where(low, none, pack),
        )
        left, right = [], []
        for number in range(4):
            kind = number // 2
            prob = jnp.exp2(score_ref[number, here] * scales[kind] - tops[kind])
            sums[kind] = sums[kind] + jnp.sum(prob.reshape(-1, 8, queries), axis=0)
            high = prob.astype(BF16)
            left += [keys[number], keys[number]]
            right += [high, (prob - high.astype(F32)).astype(BF16)]
        means = means + lax.dot_general(
            jnp.concatenate(left, axis=0),
            jnp.concatenate(right, axis=0),
            (((0,), (0,)), ((), ())),
            preferred_element_type=F32,
        )
        return sums[0], sums[1], means

    none = jnp.zeros((8, queries), F32)
    state = lax.fori_loop(
        0, steps, gather, (none, none, jnp.zeros((LANES, queries), F32)), unroll=True
    )
    lines, columns = [], []
    for kind in range(2):
        total = jnp.sum(state[kind], axis=0, keepdims=True)
        log = tops[kind] + jnp.log2(total)
        lines += [log[:, k : k + LANES] for k in range(0, queries, LANES)]
        mean = state[2][kind * HALF : kind * HALF + SH] * (1.0 / total)
        columns += [mean, jnp.broadcast_to(log, (HALF - SH, queries))]
    groups, own = out_ref.shape[0], out_ref.shape[1] - 8
    means = jnp.concatenate(columns, axis=0).T.reshape(groups, queries // groups, LANES)
    out_ref[:, :own, :] = squeeze(means)
    out_ref[:, own:, :] = jnp.broadcast_to(
        jnp.concatenate(lines, axis=0)[None], (groups, 8, LANES)
    )


def grads_kernel(
    chunk, near_ref, core_ref, logs_ref, weights_ref, own_ref, keys_ref, span_ref, key_ref,
    own_out_ref, mean_ref,
):
    deep = logs_ref.shape[1] - 8
    logs = logs_ref[:, deep:, :]
    high = jnp.max(logs, axis=0)
    logs = high + jnp.log2(jnp.sum(jnp.exp2(logs - high[None]), axis=0))
    lines = logs.shape[0] // 2
    flat = lambda rows: jnp.concatenate([rows[k : k + 1] for k in range(lines)], axis=1)
    teach_log, stud_log = flat(logs[:lines]), flat(logs[lines:])
    weights = weights_ref[...]
    own = key_ref.shape[1]

    found = []
    for part in spread(logs_ref[:, :deep, :]):
        each = part[:, :, SH : SH + 1]
        share = jnp.exp2(each - jnp.max(each, axis=0, keepdims=True))
        found.append(jnp.sum(share * part, axis=0) / jnp.sum(share, axis=0))
    mean = (found[1] - found[0]) * own_ref[:, :UNIT] * (1.0 / math.sqrt(SH))
    mean = jnp.concatenate([mean, jnp.zeros((mean.shape[0], LANES - UNIT), F32)], axis=1)
    mean_ref[...] = mean.reshape(mean_ref.shape)
    spot = near_ref[0] * CORES + core_ref[0]
    for step_to in range(NEAR * CORES):
        own_out_ref[step_to] = mean_ref[spot ^ step_to]

    def grad(teach_score, stud_score):
        teach = jnp.exp2(teach_score * (LOG2E / math.sqrt(TH)) - teach_log)
        stud = jnp.exp2(stud_score * (LOG2E / math.sqrt(SH)) - stud_log)
        return (weights * (stud - teach)).astype(BF16)

    def step(index, _):
        first, second, pack = key_chunk(keys_ref, index * chunk, chunk)
        left = grad(scores_of(span_ref[0], first), scores_of(span_ref[1], pack))
        right = grad(scores_of(span_ref[0], second), scores_of(span_ref[2], pack))
        mix = jnp.dot(left, span_ref[1], preferred_element_type=F32)
        mix = mix + jnp.dot(right, span_ref[2], preferred_element_type=F32)
        mix = (mix * (1.0 / math.sqrt(SH))).astype(key_ref.dtype)
        key_ref[pl.ds(index * chunk, chunk)] = mix.reshape(chunk, own, LANES)
        return 0

    lax.fori_loop(0, keys_ref.shape[0] // chunk, step, 0, unroll=True)


def unpack_keys(turn_ref, in_ref, out_ref):
    half = in_ref.shape[1]
    group = 16
    for start in range(0, in_ref.shape[0], group):
        for side in range(2):
            parts = [
                in_ref[head ^ turn_ref[0], :, side * HALF : side * HALF + SH].astype(F32)
                for head in range(start, start + group)
            ]
            out_ref[side * half : (side + 1) * half, start * SH : (start + group) * SH] = (
                jnp.concatenate(parts, axis=1)
            )


def unpack_rows(near_ref, core_ref, turn_ref, mine_ref, along_ref, across_ref, out_ref, part_ref):
    spot = (near_ref[0] * CORES + core_ref[0]) ^ turn_ref[0]
    part_ref[spot] = mine_ref[0]
    part_ref[spot ^ 2] = along_ref[0]
    part_ref[spot ^ 1] = across_ref[0]
    part_ref[spot ^ 3] = across_ref[1]
    out_ref[...] = jnp.concatenate(
        [part_ref[head, :, :SH] for head in range(part_ref.shape[0])], axis=1
    )


def call(body, shapes, scratch=(), smem=0, raw=0, raw_out=0, flops=0, room=48):
    kinds = [pltpu.SMEM, pltpu.HBM, pltpu.VMEM]
    specs = lambda counts: [
        pl.BlockSpec(memory_space=kind) for kind, count in zip(kinds, counts) for _ in range(count)
    ]

    def run(*args):
        many = isinstance(shapes, (list, tuple))
        outs = specs((0, raw_out, (len(shapes) if many else 1) - raw_out))
        moved = sum(arg.size * arg.dtype.itemsize for arg in args)
        return pl.pallas_call(
            body,
            out_shape=shapes,
            in_specs=specs((smem, raw, len(args) - smem - raw)),
            out_specs=outs if many else outs[0],
            scratch_shapes=list(scratch),
            cost_estimate=pl.CostEstimate(flops=flops, bytes_accessed=moved, transcendentals=0),
            compiler_params=pltpu.CompilerParams(vmem_limit_bytes=room * 2**20),
        )(*args)

    return run


def alternate(places):
    return [[z * CORES + (core ^ flip) for z, core in places] for flip in range(CORES)]


def on_device(teacher_span, teacher_context, student_span, student_context, query_weights):
    groups, tps = lax.axis_size("group"), lax.axis_size("tp")
    heads = tps * NEAR * CORES
    near = NEAR * CORES
    rows_own, tokens_own = teacher_span.shape[0], teacher_context.shape[0]
    half = tokens_own // 2
    queries = query_weights.shape[0]
    shape = jax.ShapeDtypeStruct

    def trade(array, axes):
        return lax.all_to_all(array, axes, split_axis=0, concat_axis=0, tiled=True)

    core = lax.axis_index("core").astype(jnp.int32)
    side = core.reshape(1)
    odd = (lax.axis_index("group") % 2).astype(jnp.int32).reshape(1)
    spot = lax.axis_index("near").astype(jnp.int32).reshape(1)
    piece = shape(((NEAR + 1) * rows_own, LANES), BF16)
    keys, kept, given = call(
        pack,
        (shape((heads, 3 * half, LANES), BF16), piece, piece),
        scratch=[
            pltpu.VMEM(teacher_span.shape, BF16),
            pltpu.VMEM(teacher_context.shape, BF16),
            pltpu.VMEM(student_span.shape, BF16),
            pltpu.VMEM(student_context.shape, BF16),
            pltpu.VMEM((heads, 3 * half, LANES), BF16),
            pltpu.SemaphoreType.DMA((8,)),
        ],
        smem=2,
        raw=4,
        raw_out=1,
        room=62,
    )(
        spot ^ side ^ odd,
        odd,
        teacher_span,
        teacher_context,
        student_span,
        student_context,
    )
    other = lax.ppermute(given, "core", [(0, 1), (1, 0)])
    order = lambda first, second: jnp.stack(
        [part.reshape(NEAR + 1, rows_own, LANES) for part in (first, second)], axis=1
    )
    shard = jnp.where(core == 0, order(kept, other), order(other, kept))
    shard = shard.reshape(1, (NEAR + 1) * CORES * rows_own, LANES)
    keys = trade(keys, ("tp", "near", "core"))
    rows = lax.all_gather(
        shard,
        ("group", "near", "core"),
        axis=0,
        tiled=True,
        axis_index_groups=alternate(
            [(z, z % NEAR ^ z // NEAR % 2) for z in range(groups * NEAR)]
        ),
    )

    deep = queries // groups
    logs, spans = call(
        functools.partial(totals_kernel, 8, 32),
        (shape((groups, 3 * deep // 4 + 8, LANES), F32), shape((3, queries, LANES), BF16)),
        scratch=[pltpu.VMEM((4, heads * half, queries), F32)],
        smem=1,
        flops=2**31,
    )(spot, keys, rows)
    logs = lax.all_to_all(
        logs,
        ("group", "near", "core"),
        split_axis=0,
        concat_axis=0,
        tiled=True,
        axis_index_groups=[
            members
            for spot_in in range(NEAR)
            for members in alternate([(z * NEAR + spot_in, z % 2) for z in range(groups)])
        ],
    )
    tokens_all = tokens_own * heads * groups
    weights = math.sqrt(tokens_all) * query_weights
    own = lax.dynamic_slice(weights, (lax.axis_index("group") * deep,), (deep,))
    own = jnp.broadcast_to(own[:, None], (deep, LANES))
    parts, mine = call(
        functools.partial(grads_kernel, 32),
        (shape((heads, half, LANES), BF16), shape((near, rows_own, LANES), F32)),
        scratch=[pltpu.VMEM((near, rows_own, LANES), F32)],
        smem=2,
        flops=2**30,
    )(spot, side, logs, weights.reshape(1, queries), own, keys, spans)
    parts = trade(parts, ("tp", "near", "core"))
    flip = lambda array, axis: lax.ppermute(array, axis, [(0, 1), (1, 0)])
    along = flip(mine[CORES:], "near")
    across = flip(jnp.stack([mine[1], along[1]]), "core")
    grad_span = call(
        unpack_rows,
        shape((rows_own, near * SH), F32),
        scratch=[pltpu.VMEM((near, rows_own, LANES), F32)],
        smem=3,
    )(spot, side, odd, mine, along, across)
    grad_context = call(unpack_keys, shape((tokens_own, heads * SH), F32), smem=1)(odd, parts)
    return (grad_span, grad_context)


def solution(mesh):
    ctx, tp = mesh.devices.shape
    split = Mesh(
        mesh.devices.reshape(ctx // (NEAR * CORES), NEAR, CORES, tp),
        ("group", "near", "core", "tp"),
    )
    rows = ("group", "near", "core")
    tokens = rows + ("tp",)
    placed = (P(rows, "tp"), P(tokens, None), P(rows, "tp"), P(tokens, None), P())
    return jax.shard_map(
        on_device,
        mesh=split,
        in_specs=placed,
        out_specs=(P(rows, "tp"), P(tokens, None)),
        check_vma=False,
    )
```

```python
import functools
import math

import jax
import jax.numpy as jnp
from jax import lax
from jax.experimental import pallas as pl
from jax.experimental.pallas import tpu as pltpu
from jax.sharding import Mesh, PartitionSpec as P

TH = 128
SH = 40
CORES = 2
NEAR = 2
LANES = 128
HALF = LANES // 2
LOG2E = math.log2(math.e)
F32 = jnp.float32
BF16 = jnp.bfloat16


def side_by_side(low, high):
    gap = jnp.zeros((low.shape[0], HALF - SH), low.dtype)
    return jnp.concatenate([low, gap, high, gap], axis=1)


def pack(side_ref, turn_ref, tq_hbm, tk_hbm, sq_hbm, sk_hbm, keys_hbm, kept_ref, given_ref,
         tq_ref, tk_ref, sq_ref, sk_ref, keys_ref, sems):
    heads, tokens, half = keys_hbm.shape[0], tk_hbm.shape[0], tk_hbm.shape[0] // 2
    fetches = [
        pltpu.make_async_copy(source, target, sems.at[number])
        for number, (source, target) in enumerate(
            [(tq_hbm, tq_ref), (sq_hbm, sq_ref), (sk_hbm, sk_ref), (tk_hbm, tk_ref)]
        )
    ]
    for copy in fetches:
        copy.start()
    rows = tq_ref.shape[0]

    def fill(out_ref, second):
        teach = [tq_ref[:, head * TH : (head + 1) * TH] for head in range(NEAR * CORES)]
        out_ref[:rows, :] = jnp.where(second, teach[1], teach[0])
        out_ref[rows : 2 * rows, :] = jnp.where(second, teach[2], teach[3])
        stud = [sq_ref[:, head * SH : (head + 1) * SH] for head in range(NEAR * CORES)]
        out_ref[2 * rows :, :] = jnp.where(
            second, side_by_side(stud[1], stud[2]), side_by_side(stud[0], stud[3])
        )

    fetches[0].wait()
    fetches[1].wait()
    second = side_ref[0] == 1
    fill(kept_ref, second)
    fill(given_ref, jnp.logical_not(second))
    fetches[2].wait()
    for head in range(heads):
        part = sk_ref[:, head * SH : (head + 1) * SH]
        keys_ref[head ^ turn_ref[0], tokens:, :] = side_by_side(part[:half], part[half:])
    fetches[3].wait()
    group = heads // 4
    sends = []
    for start in range(0, heads, group):
        for head in range(start, start + group):
            keys_ref[head ^ turn_ref[0], :tokens, :] = tk_ref[:, head * TH : (head + 1) * TH]
        here = pl.ds(start, group)
        sends.append(
            pltpu.make_async_copy(keys_ref.at[here], keys_hbm.at[here], sems.at[4 + start // group])
        )
        sends[-1].start()
    for copy in sends:
        copy.wait()


def queries_of(near_ref, rows_ref):
    count, deep, lanes = rows_ref.shape
    own = deep // (NEAR + 1)
    near = near_ref[0]
    start = pl.multiple_of(near * own, own)
    teach = rows_ref[:, pl.ds(start, own), :].reshape(count * own, lanes)
    stud = rows_ref[:, NEAR * own :, :].reshape(count * own, lanes).astype(F32)
    turned = jnp.concatenate([stud[:, HALF:], stud[:, :HALF]], axis=1)
    low = lax.broadcasted_iota(jnp.int32, (1, lanes), 1) < HALF
    first = near == 0
    left = jnp.where(low, jnp.where(first, stud, turned), 0.0)
    right = jnp.where(low, 0.0, jnp.where(first, turned, stud))
    return teach, left.astype(BF16), right.astype(BF16)


def key_chunk(keys_ref, start, size):
    part = keys_ref[pl.ds(start, size)]
    own = part.shape[1] // 3
    flat = lambda block: block.reshape(size * own, LANES)
    return flat(part[:, :own]), flat(part[:, own : 2 * own]), flat(part[:, 2 * own :])


def scores_of(span, key):
    return lax.dot_general(key, span, (((1,), (1,)), ((), ())), preferred_element_type=F32)


def turn(array):
    return jnp.concatenate([array[..., HALF:], array[..., :HALF]], axis=-1)


def low_lanes(rank):
    shape = (1,) * (rank - 1) + (LANES,)
    return lax.broadcasted_iota(jnp.int32, shape, rank - 1) < HALF


UNIT = SH + 2


def squeeze(means):
    teach, stud = means[:, :, :UNIT], means[:, :, HALF : HALF + UNIT]
    rows = means.shape[1]
    deep = 3 * rows // 4
    rest = rows - (deep - (rows - deep))
    none = jnp.zeros_like(stud[:, : deep - rest])
    second = jnp.concatenate([teach[:, deep:], stud[:, : rows - rest]], axis=1)
    third = jnp.concatenate([stud[:, rows - rest :], none], axis=1)
    gap = jnp.zeros(third.shape[:2] + (LANES - 3 * UNIT,), F32)
    return jnp.concatenate([teach[:, :deep], second, third, gap], axis=2)


def spread(packed):
    deep = packed.shape[1]
    rows = deep * 4 // 3
    rest = rows - (deep - (rows - deep))
    first, second, third = (packed[:, :, k * UNIT : (k + 1) * UNIT] for k in range(3))
    teach = jnp.concatenate([first, second[:, : rows - deep]], axis=1)
    stud = jnp.concatenate([second[:, rows - deep :], third[:, :rest]], axis=1)
    return teach, stud


def totals_kernel(chunk, near_ref, keys_ref, rows_ref, out_ref, span_ref):
    teach_q, left_q, right_q = queries_of(near_ref, rows_ref)
    span_ref[0], span_ref[1], span_ref[2] = teach_q, left_q, right_q
    queries = teach_q.shape[0]
    scales = (LOG2E / math.sqrt(TH), LOG2E / math.sqrt(SH))

    def step(index, state):
        old, sums, means = state[:2], list(state[2:4]), state[4]
        first, second, pack = key_chunk(keys_ref, index * chunk, chunk)
        scores = [
            scores_of(span_ref[span], key) * scales[span > 0]
            for span, key in ((0, first), (0, second), (1, pack), (2, pack))
        ]
        tops = [
            jnp.maximum(
                old[kind],
                jnp.max(
                    jnp.maximum(scores[2 * kind], scores[2 * kind + 1]), axis=0, keepdims=True
                ),
            )
            for kind in range(2)
        ]
        fades = [jnp.exp2(old[kind] - tops[kind]) for kind in range(2)]
        low = low_lanes(2)
        none = jnp.zeros_like(pack)
        turned = turn(pack.astype(F32)).astype(BF16)
        keys = (
            jnp.where(low, pack, none),
            jnp.where(low, turned, none),
            jnp.where(low, none, turned),
            jnp.where(low, none, pack),
        )
        left, right = [], []
        for number in range(4):
            kind = number // 2
            if number % 2 == 0:
                sums[kind] = sums[kind] * fades[kind]
            prob = jnp.exp2(scores[number] - tops[kind])
            sums[kind] = sums[kind] + jnp.sum(prob.reshape(-1, 8, queries), axis=0)
            high = prob.astype(BF16)
            left += [keys[number], keys[number]]
            right += [high, (prob - high.astype(F32)).astype(BF16)]
        fade = jnp.concatenate([jnp.broadcast_to(row, (HALF, queries)) for row in fades], axis=0)
        means = means * fade + lax.dot_general(
            jnp.concatenate(left, axis=0),
            jnp.concatenate(right, axis=0),
            (((0,), (0,)), ((), ())),
            preferred_element_type=F32,
        )
        return *tops, *sums, means

    lowest = jnp.full((1, queries), -1e30, F32)
    none = jnp.zeros((8, queries), F32)
    state = (lowest, lowest, none, none, jnp.zeros((LANES, queries), F32))
    state = lax.fori_loop(0, keys_ref.shape[0] // chunk, step, state, unroll=True)
    tops, state = state[:2], state[2:]
    lines, columns = [], []
    for kind in range(2):
        total = jnp.sum(state[kind], axis=0, keepdims=True)
        log = tops[kind] + jnp.log2(total)
        lines += [log[:, k : k + LANES] for k in range(0, queries, LANES)]
        mean = state[2][kind * HALF : kind * HALF + SH] * (1.0 / total)
        columns += [mean, jnp.broadcast_to(log, (HALF - SH, queries))]
    groups, own = out_ref.shape[0], out_ref.shape[1] - 8
    means = jnp.concatenate(columns, axis=0).T.reshape(groups, queries // groups, LANES)
    out_ref[:, :own, :] = squeeze(means)
    out_ref[:, own:, :] = jnp.broadcast_to(
        jnp.concatenate(lines, axis=0)[None], (groups, 8, LANES)
    )


def grads_kernel(
    chunk, near_ref, core_ref, logs_ref, weights_ref, own_ref, keys_ref, span_ref, key_ref,
    own_out_ref, mean_ref,
):
    deep = logs_ref.shape[1] - 8
    logs = logs_ref[:, deep:, :]
    high = jnp.max(logs, axis=0)
    logs = high + jnp.log2(jnp.sum(jnp.exp2(logs - high[None]), axis=0))
    lines = logs.shape[0] // 2
    flat = lambda rows: jnp.concatenate([rows[k : k + 1] for k in range(lines)], axis=1)
    teach_log, stud_log = flat(logs[:lines]), flat(logs[lines:])
    weights = weights_ref[...]
    own = key_ref.shape[1]

    found = []
    for part in spread(logs_ref[:, :deep, :]):
        each = part[:, :, SH : SH + 1]
        share = jnp.exp2(each - jnp.max(each, axis=0, keepdims=True))
        found.append(jnp.sum(share * part, axis=0) / jnp.sum(share, axis=0))
    mean = (found[1] - found[0]) * own_ref[:, :UNIT] * (1.0 / math.sqrt(SH))
    mean = jnp.concatenate([mean, jnp.zeros((mean.shape[0], LANES - UNIT), F32)], axis=1)
    mean_ref[...] = mean.reshape(mean_ref.shape)
    spot = near_ref[0] * CORES + core_ref[0]
    for step_to in range(NEAR * CORES):
        own_out_ref[step_to] = mean_ref[spot ^ step_to]

    def grad(teach_score, stud_score):
        teach = jnp.exp2(teach_score * (LOG2E / math.sqrt(TH)) - teach_log)
        stud = jnp.exp2(stud_score * (LOG2E / math.sqrt(SH)) - stud_log)
        return (weights * (stud - teach)).astype(BF16)

    def step(index, _):
        first, second, pack = key_chunk(keys_ref, index * chunk, chunk)
        left = grad(scores_of(span_ref[0], first), scores_of(span_ref[1], pack))
        right = grad(scores_of(span_ref[0], second), scores_of(span_ref[2], pack))
        mix = jnp.dot(left, span_ref[1], preferred_element_type=F32)
        mix = mix + jnp.dot(right, span_ref[2], preferred_element_type=F32)
        mix = (mix * (1.0 / math.sqrt(SH))).astype(key_ref.dtype)
        key_ref[pl.ds(index * chunk, chunk)] = mix.reshape(chunk, own, LANES)
        return 0

    lax.fori_loop(0, keys_ref.shape[0] // chunk, step, 0, unroll=True)


def unpack_keys(turn_ref, in_ref, out_ref):
    half = in_ref.shape[1]
    group = 16
    for start in range(0, in_ref.shape[0], group):
        for side in range(2):
            parts = [
                in_ref[head ^ turn_ref[0], :, side * HALF : side * HALF + SH].astype(F32)
                for head in range(start, start + group)
            ]
            out_ref[side * half : (side + 1) * half, start * SH : (start + group) * SH] = (
                jnp.concatenate(parts, axis=1)
            )


def unpack_rows(near_ref, core_ref, turn_ref, mine_ref, along_ref, across_ref, out_ref, part_ref):
    spot = (near_ref[0] * CORES + core_ref[0]) ^ turn_ref[0]
    part_ref[spot] = mine_ref[0]
    part_ref[spot ^ 2] = along_ref[0]
    part_ref[spot ^ 1] = across_ref[0]
    part_ref[spot ^ 3] = across_ref[1]
    out_ref[...] = jnp.concatenate(
        [part_ref[head, :, :SH] for head in range(part_ref.shape[0])], axis=1
    )


def call(body, shapes, scratch=(), smem=0, raw=0, raw_out=0, flops=0, room=48):
    kinds = [pltpu.SMEM, pltpu.HBM, pltpu.VMEM]
    specs = lambda counts: [
        pl.BlockSpec(memory_space=kind) for kind, count in zip(kinds, counts) for _ in range(count)
    ]

    def run(*args):
        many = isinstance(shapes, (list, tuple))
        outs = specs((0, raw_out, (len(shapes) if many else 1) - raw_out))
        moved = sum(arg.size * arg.dtype.itemsize for arg in args)
        return pl.pallas_call(
            body,
            out_shape=shapes,
            in_specs=specs((smem, raw, len(args) - smem - raw)),
            out_specs=outs if many else outs[0],
            scratch_shapes=list(scratch),
            cost_estimate=pl.CostEstimate(flops=flops, bytes_accessed=moved, transcendentals=0),
            compiler_params=pltpu.CompilerParams(vmem_limit_bytes=room * 2**20),
        )(*args)

    return run


def alternate(places):
    return [[z * CORES + (core ^ flip) for z, core in places] for flip in range(CORES)]


def on_device(teacher_span, teacher_context, student_span, student_context, query_weights):
    groups, tps = lax.axis_size("group"), lax.axis_size("tp")
    heads = tps * NEAR * CORES
    near = NEAR * CORES
    rows_own, tokens_own = teacher_span.shape[0], teacher_context.shape[0]
    half = tokens_own // 2
    queries = query_weights.shape[0]
    shape = jax.ShapeDtypeStruct

    def trade(array, axes):
        return lax.all_to_all(array, axes, split_axis=0, concat_axis=0, tiled=True)

    core = lax.axis_index("core").astype(jnp.int32)
    side = core.reshape(1)
    odd = (lax.axis_index("group") % 2).astype(jnp.int32).reshape(1)
    spot = lax.axis_index("near").astype(jnp.int32).reshape(1)
    piece = shape(((NEAR + 1) * rows_own, LANES), BF16)
    keys, kept, given = call(
        pack,
        (shape((heads, 3 * half, LANES), BF16), piece, piece),
        scratch=[
            pltpu.VMEM(teacher_span.shape, BF16),
            pltpu.VMEM(teacher_context.shape, BF16),
            pltpu.VMEM(student_span.shape, BF16),
            pltpu.VMEM(student_context.shape, BF16),
            pltpu.VMEM((heads, 3 * half, LANES), BF16),
            pltpu.SemaphoreType.DMA((8,)),
        ],
        smem=2,
        raw=4,
        raw_out=1,
        room=62,
    )(
        spot ^ side ^ odd,
        odd,
        teacher_span,
        teacher_context,
        student_span,
        student_context,
    )
    other = lax.ppermute(given, "core", [(0, 1), (1, 0)])
    order = lambda first, second: jnp.stack(
        [part.reshape(NEAR + 1, rows_own, LANES) for part in (first, second)], axis=1
    )
    shard = jnp.where(core == 0, order(kept, other), order(other, kept))
    shard = shard.reshape(1, (NEAR + 1) * CORES * rows_own, LANES)
    keys = trade(keys, ("tp", "near", "core"))
    rows = lax.all_gather(
        shard,
        ("group", "near", "core"),
        axis=0,
        tiled=True,
        axis_index_groups=alternate(
            [(z, z % NEAR ^ z // NEAR % 2) for z in range(groups * NEAR)]
        ),
    )

    deep = queries // groups
    logs, spans = call(
        functools.partial(totals_kernel, 8),
        (shape((groups, 3 * deep // 4 + 8, LANES), F32), shape((3, queries, LANES), BF16)),
        smem=1,
        flops=2**31,
    )(spot, keys, rows)
    logs = lax.all_to_all(
        logs,
        ("group", "near", "core"),
        split_axis=0,
        concat_axis=0,
        tiled=True,
        axis_index_groups=[
            members
            for spot_in in range(NEAR)
            for members in alternate([(z * NEAR + spot_in, z % 2) for z in range(groups)])
        ],
    )
    tokens_all = tokens_own * heads * groups
    weights = math.sqrt(tokens_all) * query_weights
    own = lax.dynamic_slice(weights, (lax.axis_index("group") * deep,), (deep,))
    own = jnp.broadcast_to(own[:, None], (deep, LANES))
    parts, mine = call(
        functools.partial(grads_kernel, 32),
        (shape((heads, half, LANES), BF16), shape((near, rows_own, LANES), F32)),
        scratch=[pltpu.VMEM((near, rows_own, LANES), F32)],
        smem=2,
        flops=2**30,
    )(spot, side, logs, weights.reshape(1, queries), own, keys, spans)
    parts = trade(parts, ("tp", "near", "core"))
    flip = lambda array, axis: lax.ppermute(array, axis, [(0, 1), (1, 0)])
    along = flip(mine[CORES:], "near")
    across = flip(jnp.stack([mine[1], along[1]]), "core")
    grad_span = call(
        unpack_rows,
        shape((rows_own, near * SH), F32),
        scratch=[pltpu.VMEM((near, rows_own, LANES), F32)],
        smem=3,
    )(spot, side, odd, mine, along, across)
    grad_context = call(unpack_keys, shape((tokens_own, heads * SH), F32), smem=1)(odd, parts)
    return (grad_span, grad_context)


def solution(mesh):
    ctx, tp = mesh.devices.shape
    split = Mesh(
        mesh.devices.reshape(ctx // (NEAR * CORES), NEAR, CORES, tp),
        ("group", "near", "core", "tp"),
    )
    rows = ("group", "near", "core")
    tokens = rows + ("tp",)
    placed = (P(rows, "tp"), P(tokens, None), P(rows, "tp"), P(tokens, None), P())
    return jax.shard_map(
        on_device,
        mesh=split,
        in_specs=placed,
        out_specs=(P(rows, "tp"), P(tokens, None)),
        check_vma=False,
    )
```

```python
import functools
import math

import jax
import jax.numpy as jnp
from jax import lax
from jax.experimental import pallas as pl
from jax.experimental.pallas import tpu as pltpu
from jax.sharding import Mesh, PartitionSpec as P

TH = 128
SH = 40
CORES = 2
NEAR = 2
LANES = 128
HALF = LANES // 2
LOG2E = math.log2(math.e)
F32 = jnp.float32
BF16 = jnp.bfloat16


def side_by_side(low, high):
    gap = jnp.zeros((low.shape[0], HALF - SH), low.dtype)
    return jnp.concatenate([low, gap, high, gap], axis=1)


def pack(side_ref, turn_ref, tq_hbm, tk_hbm, sq_hbm, sk_hbm, keys_hbm, kept_ref, given_ref,
         tq_ref, tk_ref, sq_ref, sk_ref, keys_ref, sems):
    heads, tokens, half = keys_hbm.shape[0], tk_hbm.shape[0], tk_hbm.shape[0] // 2
    fetches = [
        pltpu.make_async_copy(source, target, sems.at[number])
        for number, (source, target) in enumerate(
            [(tq_hbm, tq_ref), (sq_hbm, sq_ref), (sk_hbm, sk_ref), (tk_hbm, tk_ref)]
        )
    ]
    for copy in fetches:
        copy.start()
    rows = tq_ref.shape[0]

    def fill(out_ref, second):
        teach = [tq_ref[:, head * TH : (head + 1) * TH] for head in range(NEAR * CORES)]
        out_ref[:rows, :] = jnp.where(second, teach[1], teach[0])
        out_ref[rows : 2 * rows, :] = jnp.where(second, teach[2], teach[3])
        stud = [sq_ref[:, head * SH : (head + 1) * SH] for head in range(NEAR * CORES)]
        out_ref[2 * rows :, :] = jnp.where(
            second, side_by_side(stud[1], stud[2]), side_by_side(stud[0], stud[3])
        )

    fetches[0].wait()
    fetches[1].wait()
    second = side_ref[0] == 1
    fill(kept_ref, second)
    fill(given_ref, jnp.logical_not(second))
    fetches[2].wait()
    for head in range(heads):
        part = sk_ref[:, head * SH : (head + 1) * SH]
        keys_ref[head ^ turn_ref[0], tokens:, :] = side_by_side(part[:half], part[half:])
    fetches[3].wait()
    group = heads // 4
    sends = []
    for start in range(0, heads, group):
        for head in range(start, start + group):
            keys_ref[head ^ turn_ref[0], :tokens, :] = tk_ref[:, head * TH : (head + 1) * TH]
        here = pl.ds(start, group)
        sends.append(
            pltpu.make_async_copy(keys_ref.at[here], keys_hbm.at[here], sems.at[4 + start // group])
        )
        sends[-1].start()
    for copy in sends:
        copy.wait()


def queries_of(near_ref, rows_ref):
    count, deep, lanes = rows_ref.shape
    own = deep // (NEAR + 1)
    near = near_ref[0]
    start = pl.multiple_of(near * own, own)
    teach = rows_ref[:, pl.ds(start, own), :].reshape(count * own, lanes)
    stud = rows_ref[:, NEAR * own :, :].reshape(count * own, lanes).astype(F32)
    turned = jnp.concatenate([stud[:, HALF:], stud[:, :HALF]], axis=1)
    low = lax.broadcasted_iota(jnp.int32, (1, lanes), 1) < HALF
    first = near == 0
    left = jnp.where(low, jnp.where(first, stud, turned), 0.0)
    right = jnp.where(low, 0.0, jnp.where(first, turned, stud))
    return teach, left.astype(BF16), right.astype(BF16)


def key_chunk(keys_ref, start, size):
    part = keys_ref[pl.ds(start, size)]
    own = part.shape[1] // 3
    flat = lambda block: block.reshape(size * own, LANES)
    return flat(part[:, :own]), flat(part[:, own : 2 * own]), flat(part[:, 2 * own :])


def scores_of(span, key):
    return lax.dot_general(key, span, (((1,), (1,)), ((), ())), preferred_element_type=F32)


def turn(array):
    return jnp.concatenate([array[..., HALF:], array[..., :HALF]], axis=-1)


def low_lanes(rank):
    shape = (1,) * (rank - 1) + (LANES,)
    return lax.broadcasted_iota(jnp.int32, shape, rank - 1) < HALF


UNIT = SH + 2


def squeeze(means):
    teach, stud = means[:, :, :UNIT], means[:, :, HALF : HALF + UNIT]
    rows = means.shape[1]
    deep = 3 * rows // 4
    rest = rows - (deep - (rows - deep))
    none = jnp.zeros_like(stud[:, : deep - rest])
    second = jnp.concatenate([teach[:, deep:], stud[:, : rows - rest]], axis=1)
    third = jnp.concatenate([stud[:, rows - rest :], none], axis=1)
    gap = jnp.zeros(third.shape[:2] + (LANES - 3 * UNIT,), F32)
    return jnp.concatenate([teach[:, :deep], second, third, gap], axis=2)


def spread(packed):
    deep = packed.shape[1]
    rows = deep * 4 // 3
    rest = rows - (deep - (rows - deep))
    first, second, third = (packed[:, :, k * UNIT : (k + 1) * UNIT] for k in range(3))
    teach = jnp.concatenate([first, second[:, : rows - deep]], axis=1)
    stud = jnp.concatenate([second[:, rows - deep :], third[:, :rest]], axis=1)
    return teach, stud


def totals_kernel(chunk, wide, near_ref, keys_ref, rows_ref, out_ref, span_ref, score_ref):
    teach_q, left_q, right_q = queries_of(near_ref, rows_ref)
    span_ref[0], span_ref[1], span_ref[2] = teach_q, left_q, right_q
    queries = teach_q.shape[0]
    steps = keys_ref.shape[0] // chunk
    scales = (LOG2E / math.sqrt(TH), LOG2E / math.sqrt(SH))

    def measure(index, tops):
        first, second, pack = key_chunk(keys_ref, index * wide, wide)
        here = pl.ds(index * first.shape[0], first.shape[0])
        found = []
        for kind, span, key in ((0, 0, first), (0, 0, second), (1, 1, pack), (1, 2, pack)):
            score = scores_of(span_ref[span], key)
            score_ref[len(found), here] = score
            found.append(jnp.max(score.reshape(-1, 8, queries), axis=0))
        return jnp.maximum(tops[0], jnp.maximum(found[0], found[1])), jnp.maximum(
            tops[1], jnp.maximum(found[2], found[3])
        )

    start = jnp.full((8, queries), -1e30, F32)
    tops = lax.fori_loop(0, keys_ref.shape[0] // wide, measure, (start, start), unroll=True)
    tops = [jnp.max(top, axis=0, keepdims=True) * scale for top, scale in zip(tops, scales)]

    def gather(index, state):
        sums, means = list(state[:2]), state[2]
        _, _, pack = key_chunk(keys_ref, index * chunk, chunk)
        here = pl.ds(index * pack.shape[0], pack.shape[0])
        low = low_lanes(2)
        none = jnp.zeros_like(pack)
        turned = turn(pack.astype(F32)).astype(BF16)
        keys = (
            jnp.where(low, pack, none),
            jnp.where(low, turned, none),
            jnp.where(low, none, turned),
            jnp.where(low, none, pack),
        )
        left, right = [], []
        for number in range(4):
            kind = number // 2
            prob = jnp.exp2(score_ref[number, here] * scales[kind] - tops[kind])
            sums[kind] = sums[kind] + jnp.sum(prob.reshape(-1, 8, queries), axis=0)
            high = prob.astype(BF16)
            left += [keys[number], keys[number]]
            right += [high, (prob - high.astype(F32)).astype(BF16)]
        means = means + lax.dot_general(
            jnp.concatenate(left, axis=0),
            jnp.concatenate(right, axis=0),
            (((0,), (0,)), ((), ())),
            preferred_element_type=F32,
        )
        return sums[0], sums[1], means

    none = jnp.zeros((8, queries), F32)
    state = lax.fori_loop(
        0, steps, gather, (none, none, jnp.zeros((LANES, queries), F32)), unroll=True
    )
    lines, columns = [], []
    for kind in range(2):
        total = jnp.sum(state[kind], axis=0, keepdims=True)
        log = tops[kind] + jnp.log2(total)
        lines += [log[:, k : k + LANES] for k in range(0, queries, LANES)]
        mean = state[2][kind * HALF : kind * HALF + SH] * (1.0 / total)
        columns += [mean, jnp.broadcast_to(log, (HALF - SH, queries))]
    groups, own = out_ref.shape[0], out_ref.shape[1] - 8
    means = jnp.concatenate(columns, axis=0).T.reshape(groups, queries // groups, LANES)
    out_ref[:, :own, :] = squeeze(means)
    out_ref[:, own:, :] = jnp.broadcast_to(
        jnp.concatenate(lines, axis=0)[None], (groups, 8, LANES)
    )


def grads_kernel(
    chunk, near_ref, core_ref, logs_ref, weights_ref, own_ref, keys_ref, span_ref, key_ref,
    own_out_ref, mean_ref,
):
    deep = logs_ref.shape[1] - 8
    logs = logs_ref[:, deep:, :]
    high = jnp.max(logs, axis=0)
    logs = high + jnp.log2(jnp.sum(jnp.exp2(logs - high[None]), axis=0))
    lines = logs.shape[0] // 2
    flat = lambda rows: jnp.concatenate([rows[k : k + 1] for k in range(lines)], axis=1)
    teach_log, stud_log = flat(logs[:lines]), flat(logs[lines:])
    weights = weights_ref[...]
    own = key_ref.shape[1]

    found = []
    for part in spread(logs_ref[:, :deep, :]):
        each = part[:, :, SH : SH + 1]
        share = jnp.exp2(each - jnp.max(each, axis=0, keepdims=True))
        found.append(jnp.sum(share * part, axis=0) / jnp.sum(share, axis=0))
    mean = (found[1] - found[0]) * own_ref[:, :UNIT] * (1.0 / math.sqrt(SH))
    mean = jnp.concatenate([mean, jnp.zeros((mean.shape[0], LANES - UNIT), F32)], axis=1)
    mean_ref[...] = mean.reshape(mean_ref.shape)
    spot = near_ref[0] * CORES + core_ref[0]
    for step_to in range(NEAR * CORES):
        own_out_ref[step_to] = mean_ref[spot ^ step_to]

    def grad(teach_score, stud_score):
        teach = jnp.exp2(teach_score * (LOG2E / math.sqrt(TH)) - teach_log)
        stud = jnp.exp2(stud_score * (LOG2E / math.sqrt(SH)) - stud_log)
        return (weights * (stud - teach)).astype(BF16)

    def step(index, _):
        first, second, pack = key_chunk(keys_ref, index * chunk, chunk)
        left = grad(scores_of(span_ref[0], first), scores_of(span_ref[1], pack))
        right = grad(scores_of(span_ref[0], second), scores_of(span_ref[2], pack))
        mix = jnp.dot(left, span_ref[1], preferred_element_type=F32)
        mix = mix + jnp.dot(right, span_ref[2], preferred_element_type=F32)
        mix = (mix * (1.0 / math.sqrt(SH))).astype(key_ref.dtype)
        key_ref[pl.ds(index * chunk, chunk)] = mix.reshape(chunk, own, LANES)
        return 0

    lax.fori_loop(0, keys_ref.shape[0] // chunk, step, 0, unroll=True)


def unpack_keys(turn_ref, in_ref, out_ref):
    half = in_ref.shape[1]
    group = 16
    for start in range(0, in_ref.shape[0], group):
        for side in range(2):
            parts = [
                in_ref[head ^ turn_ref[0], :, side * HALF : side * HALF + SH].astype(F32)
                for head in range(start, start + group)
            ]
            out_ref[side * half : (side + 1) * half, start * SH : (start + group) * SH] = (
                jnp.concatenate(parts, axis=1)
            )


def unpack_rows(near_ref, core_ref, turn_ref, mine_ref, along_ref, across_ref, out_ref, part_ref):
    spot = (near_ref[0] * CORES + core_ref[0]) ^ turn_ref[0]
    part_ref[spot] = mine_ref[0]
    part_ref[spot ^ 2] = along_ref[0]
    part_ref[spot ^ 1] = across_ref[0]
    part_ref[spot ^ 3] = across_ref[1]
    out_ref[...] = jnp.concatenate(
        [part_ref[head, :, :SH] for head in range(part_ref.shape[0])], axis=1
    )


def call(body, shapes, scratch=(), smem=0, raw=0, raw_out=0, flops=0, room=48):
    kinds = [pltpu.SMEM, pltpu.HBM, pltpu.VMEM]
    specs = lambda counts: [
        pl.BlockSpec(memory_space=kind) for kind, count in zip(kinds, counts) for _ in range(count)
    ]

    def run(*args):
        many = isinstance(shapes, (list, tuple))
        outs = specs((0, raw_out, (len(shapes) if many else 1) - raw_out))
        moved = sum(arg.size * arg.dtype.itemsize for arg in args)
        return pl.pallas_call(
            body,
            out_shape=shapes,
            in_specs=specs((smem, raw, len(args) - smem - raw)),
            out_specs=outs if many else outs[0],
            scratch_shapes=list(scratch),
            cost_estimate=pl.CostEstimate(flops=flops, bytes_accessed=moved, transcendentals=0),
            compiler_params=pltpu.CompilerParams(vmem_limit_bytes=room * 2**20),
        )(*args)

    return run


def alternate(places):
    return [[z * CORES + (core ^ flip) for z, core in places] for flip in range(CORES)]


def on_device(teacher_span, teacher_context, student_span, student_context, query_weights):
    groups, tps = lax.axis_size("group"), lax.axis_size("tp")
    heads = tps * NEAR * CORES
    near = NEAR * CORES
    rows_own, tokens_own = teacher_span.shape[0], teacher_context.shape[0]
    half = tokens_own // 2
    queries = query_weights.shape[0]
    shape = jax.ShapeDtypeStruct

    def trade(array, axes):
        return lax.all_to_all(array, axes, split_axis=0, concat_axis=0, tiled=True)

    core = lax.axis_index("core").astype(jnp.int32)
    side = core.reshape(1)
    odd = (lax.axis_index("group") % 2).astype(jnp.int32).reshape(1)
    spot = lax.axis_index("near").astype(jnp.int32).reshape(1)
    piece = shape(((NEAR + 1) * rows_own, LANES), BF16)
    keys, kept, given = call(
        pack,
        (shape((heads, 3 * half, LANES), BF16), piece, piece),
        scratch=[
            pltpu.VMEM(teacher_span.shape, BF16),
            pltpu.VMEM(teacher_context.shape, BF16),
            pltpu.VMEM(student_span.shape, BF16),
            pltpu.VMEM(student_context.shape, BF16),
            pltpu.VMEM((heads, 3 * half, LANES), BF16),
            pltpu.SemaphoreType.DMA((8,)),
        ],
        smem=2,
        raw=4,
        raw_out=1,
        room=62,
    )(
        spot ^ side ^ odd,
        odd,
        teacher_span,
        teacher_context,
        student_span,
        student_context,
    )
    other = lax.ppermute(given, "core", [(0, 1), (1, 0)])
    order = lambda first, second: jnp.stack(
        [part.reshape(NEAR + 1, rows_own, LANES) for part in (first, second)], axis=1
    )
    shard = jnp.where(core == 0, order(kept, other), order(other, kept))
    shard = shard.reshape(1, (NEAR + 1) * CORES * rows_own, LANES)
    keys = trade(keys, ("tp", "near", "core"))
    rows = lax.all_gather(
        shard,
        ("group", "near", "core"),
        axis=0,
        tiled=True,
        axis_index_groups=alternate(
            [(z, z % NEAR ^ z // NEAR % 2) for z in range(groups * NEAR)]
        ),
    )

    deep = queries // groups
    logs, spans = call(
        functools.partial(totals_kernel, 16, 32),
        (shape((groups, 3 * deep // 4 + 8, LANES), F32), shape((3, queries, LANES), BF16)),
        scratch=[pltpu.VMEM((4, heads * half, queries), F32)],
        smem=1,
        flops=2**31,
    )(spot, keys, rows)
    logs = lax.all_to_all(
        logs,
        ("group", "near", "core"),
        split_axis=0,
        concat_axis=0,
        tiled=True,
        axis_index_groups=[
            members
            for spot_in in range(NEAR)
            for members in alternate([(z * NEAR + spot_in, z % 2) for z in range(groups)])
        ],
    )
    tokens_all = tokens_own * heads * groups
    weights = math.sqrt(tokens_all) * query_weights
    own = lax.dynamic_slice(weights, (lax.axis_index("group") * deep,), (deep,))
    own = jnp.broadcast_to(own[:, None], (deep, LANES))
    parts, mine = call(
        functools.partial(grads_kernel, 32),
        (shape((heads, half, LANES), BF16), shape((near, rows_own, LANES), F32)),
        scratch=[pltpu.VMEM((near, rows_own, LANES), F32)],
        smem=2,
        flops=2**30,
    )(spot, side, logs, weights.reshape(1, queries), own, keys, spans)
    parts = trade(parts, ("tp", "near", "core"))
    flip = lambda array, axis: lax.ppermute(array, axis, [(0, 1), (1, 0)])
    along = flip(mine[CORES:], "near")
    across = flip(jnp.stack([mine[1], along[1]]), "core")
    grad_span = call(
        unpack_rows,
        shape((rows_own, near * SH), F32),
        scratch=[pltpu.VMEM((near, rows_own, LANES), F32)],
        smem=3,
    )(spot, side, odd, mine, along, across)
    grad_context = call(unpack_keys, shape((tokens_own, heads * SH), F32), smem=1)(odd, parts)
    return (grad_span, grad_context)


def solution(mesh):
    ctx, tp = mesh.devices.shape
    split = Mesh(
        mesh.devices.reshape(ctx // (NEAR * CORES), NEAR, CORES, tp),
        ("group", "near", "core", "tp"),
    )
    rows = ("group", "near", "core")
    tokens = rows + ("tp",)
    placed = (P(rows, "tp"), P(tokens, None), P(rows, "tp"), P(tokens, None), P())
    return jax.shard_map(
        on_device,
        mesh=split,
        in_specs=placed,
        out_specs=(P(rows, "tp"), P(tokens, None)),
        check_vma=False,
    )
```

```python
import functools
import math

import jax
import jax.numpy as jnp
from jax import lax
from jax.experimental import pallas as pl
from jax.experimental.pallas import tpu as pltpu
from jax.sharding import Mesh, PartitionSpec as P

TH = 128
SH = 40
CORES = 2
NEAR = 2
LANES = 128
HALF = LANES // 2
LOG2E = math.log2(math.e)
F32 = jnp.float32
BF16 = jnp.bfloat16


def side_by_side(low, high):
    gap = jnp.zeros((low.shape[0], HALF - SH), low.dtype)
    return jnp.concatenate([low, gap, high, gap], axis=1)


def pack(side_ref, tq_hbm, tk_hbm, sq_hbm, sk_hbm, keys_hbm, kept_ref, given_ref,
         tq_ref, tk_ref, sq_ref, sk_ref, keys_ref, sems):
    heads, tokens, half = keys_hbm.shape[0], tk_hbm.shape[0], tk_hbm.shape[0] // 2
    fetches = [
        pltpu.make_async_copy(source, target, sems.at[number])
        for number, (source, target) in enumerate(
            [(tq_hbm, tq_ref), (sq_hbm, sq_ref), (sk_hbm, sk_ref), (tk_hbm, tk_ref)]
        )
    ]
    for copy in fetches:
        copy.start()
    rows = tq_ref.shape[0]

    def fill(out_ref, second):
        teach = [tq_ref[:, head * TH : (head + 1) * TH] for head in range(NEAR * CORES)]
        out_ref[:rows, :] = jnp.where(second, teach[1], teach[0])
        out_ref[rows : 2 * rows, :] = jnp.where(second, teach[2], teach[3])
        stud = [sq_ref[:, head * SH : (head + 1) * SH] for head in range(NEAR * CORES)]
        out_ref[2 * rows :, :] = jnp.where(
            second, side_by_side(stud[1], stud[2]), side_by_side(stud[0], stud[3])
        )

    fetches[0].wait()
    fetches[1].wait()
    second = side_ref[0] == 1
    fill(kept_ref, second)
    fill(given_ref, jnp.logical_not(second))
    fetches[2].wait()
    for head in range(heads):
        part = sk_ref[:, head * SH : (head + 1) * SH]
        keys_ref[head, tokens:, :] = side_by_side(part[:half], part[half:])
    fetches[3].wait()
    group = heads // 4
    sends = []
    for start in range(0, heads, group):
        for head in range(start, start + group):
            keys_ref[head, :tokens, :] = tk_ref[:, head * TH : (head + 1) * TH]
        here = pl.ds(start, group)
        sends.append(
            pltpu.make_async_copy(keys_ref.at[here], keys_hbm.at[here], sems.at[4 + start // group])
        )
        sends[-1].start()
    for copy in sends:
        copy.wait()


def queries_of(near_ref, rows_ref):
    count, deep, lanes = rows_ref.shape
    own = deep // (NEAR + 1)
    near = near_ref[0]
    start = pl.multiple_of(near * own, own)
    teach = rows_ref[:, pl.ds(start, own), :].reshape(count * own, lanes)
    stud = rows_ref[:, NEAR * own :, :].reshape(count * own, lanes).astype(F32)
    turned = jnp.concatenate([stud[:, HALF:], stud[:, :HALF]], axis=1)
    low = lax.broadcasted_iota(jnp.int32, (1, lanes), 1) < HALF
    first = near == 0
    left = jnp.where(low, jnp.where(first, stud, turned), 0.0)
    right = jnp.where(low, 0.0, jnp.where(first, turned, stud))
    return teach, left.astype(BF16), right.astype(BF16)


def key_chunk(keys_ref, start, size):
    part = keys_ref[pl.ds(start, size)]
    own = part.shape[1] // 3
    flat = lambda block: block.reshape(size * own, LANES)
    return flat(part[:, :own]), flat(part[:, own : 2 * own]), flat(part[:, 2 * own :])


def scores_of(span, key):
    return lax.dot_general(key, span, (((1,), (1,)), ((), ())), preferred_element_type=F32)


def turn(array):
    return jnp.concatenate([array[..., HALF:], array[..., :HALF]], axis=-1)


def low_lanes(rank):
    shape = (1,) * (rank - 1) + (LANES,)
    return lax.broadcasted_iota(jnp.int32, shape, rank - 1) < HALF


UNIT = SH + 2


def squeeze(means):
    teach, stud = means[:, :, :UNIT], means[:, :, HALF : HALF + UNIT]
    rows = means.shape[1]
    deep = 3 * rows // 4
    rest = rows - (deep - (rows - deep))
    none = jnp.zeros_like(stud[:, : deep - rest])
    second = jnp.concatenate([teach[:, deep:], stud[:, : rows - rest]], axis=1)
    third = jnp.concatenate([stud[:, rows - rest :], none], axis=1)
    gap = jnp.zeros(third.shape[:2] + (LANES - 3 * UNIT,), F32)
    return jnp.concatenate([teach[:, :deep], second, third, gap], axis=2)


def spread(packed):
    deep = packed.shape[1]
    rows = deep * 4 // 3
    rest = rows - (deep - (rows - deep))
    first, second, third = (packed[:, :, k * UNIT : (k + 1) * UNIT] for k in range(3))
    teach = jnp.concatenate([first, second[:, : rows - deep]], axis=1)
    stud = jnp.concatenate([second[:, rows - deep :], third[:, :rest]], axis=1)
    return teach, stud


def totals_kernel(chunk, wide, near_ref, keys_ref, rows_ref, out_ref, span_ref, score_ref):
    teach_q, left_q, right_q = queries_of(near_ref, rows_ref)
    span_ref[0], span_ref[1], span_ref[2] = teach_q, left_q, right_q
    queries = teach_q.shape[0]
    steps = keys_ref.shape[0] // chunk
    scales = (LOG2E / math.sqrt(TH), LOG2E / math.sqrt(SH))

    def measure(index, tops):
        first, second, pack = key_chunk(keys_ref, index * wide, wide)
        here = pl.ds(index * first.shape[0], first.shape[0])
        found = []
        for kind, span, key in ((0, 0, first), (0, 0, second), (1, 1, pack), (1, 2, pack)):
            score = scores_of(span_ref[span], key)
            score_ref[len(found), here] = score
            found.append(jnp.max(score.reshape(-1, 8, queries), axis=0))
        return jnp.maximum(tops[0], jnp.maximum(found[0], found[1])), jnp.maximum(
            tops[1], jnp.maximum(found[2], found[3])
        )

    start = jnp.full((8, queries), -1e30, F32)
    tops = lax.fori_loop(0, keys_ref.shape[0] // wide, measure, (start, start), unroll=True)
    tops = [jnp.max(top, axis=0, keepdims=True) * scale for top, scale in zip(tops, scales)]

    def gather(index, state):
        sums, means = list(state[:2]), state[2]
        _, _, pack = key_chunk(keys_ref, index * chunk, chunk)
        here = pl.ds(index * pack.shape[0], pack.shape[0])
        low = low_lanes(2)
        none = jnp.zeros_like(pack)
        turned = turn(pack.astype(F32)).astype(BF16)
        keys = (
            jnp.where(low, pack, none),
            jnp.where(low, turned, none),
            jnp.where(low, none, turned),
            jnp.where(low, none, pack),
        )
        left, right = [], []
        for number in range(4):
            kind = number // 2
            prob = jnp.exp2(score_ref[number, here] * scales[kind] - tops[kind])
            sums[kind] = sums[kind] + jnp.sum(prob.reshape(-1, 8, queries), axis=0)
            high = prob.astype(BF16)
            left += [keys[number], keys[number]]
            right += [high, (prob - high.astype(F32)).astype(BF16)]
        means = means + lax.dot_general(
            jnp.concatenate(left, axis=0),
            jnp.concatenate(right, axis=0),
            (((0,), (0,)), ((), ())),
            preferred_element_type=F32,
        )
        return sums[0], sums[1], means

    none = jnp.zeros((8, queries), F32)
    state = lax.fori_loop(
        0, steps, gather, (none, none, jnp.zeros((LANES, queries), F32)), unroll=True
    )
    lines, columns = [], []
    for kind in range(2):
        total = jnp.sum(state[kind], axis=0, keepdims=True)
        log = tops[kind] + jnp.log2(total)
        lines += [log[:, k : k + LANES] for k in range(0, queries, LANES)]
        mean = state[2][kind * HALF : kind * HALF + SH] * (1.0 / total)
        columns += [mean, jnp.broadcast_to(log, (HALF - SH, queries))]
    groups, own = out_ref.shape[0], out_ref.shape[1] - 8
    means = jnp.concatenate(columns, axis=0).T.reshape(groups, queries // groups, LANES)
    out_ref[:, :own, :] = squeeze(means)
    out_ref[:, own:, :] = jnp.broadcast_to(
        jnp.concatenate(lines, axis=0)[None], (groups, 8, LANES)
    )


def grads_kernel(
    chunk, near_ref, core_ref, logs_ref, weights_ref, own_ref, keys_ref, span_ref, key_ref,
    own_out_ref, mean_ref,
):
    deep = logs_ref.shape[1] - 8
    logs = logs_ref[:, deep:, :]
    high = jnp.max(logs, axis=0)
    logs = high + jnp.log2(jnp.sum(jnp.exp2(logs - high[None]), axis=0))
    lines = logs.shape[0] // 2
    flat = lambda rows: jnp.concatenate([rows[k : k + 1] for k in range(lines)], axis=1)
    teach_log, stud_log = flat(logs[:lines]), flat(logs[lines:])
    weights = weights_ref[...]
    own = key_ref.shape[1]

    found = []
    for part in spread(logs_ref[:, :deep, :]):
        each = part[:, :, SH : SH + 1]
        share = jnp.exp2(each - jnp.max(each, axis=0, keepdims=True))
        found.append(jnp.sum(share * part, axis=0) / jnp.sum(share, axis=0))
    mean = (found[1] - found[0]) * own_ref[:, :UNIT] * (1.0 / math.sqrt(SH))
    mean = jnp.concatenate([mean, jnp.zeros((mean.shape[0], LANES - UNIT), F32)], axis=1)
    mean_ref[...] = mean.reshape(mean_ref.shape)
    spot = near_ref[0] * CORES + core_ref[0]
    for step_to in range(NEAR * CORES):
        own_out_ref[step_to] = mean_ref[spot ^ step_to]

    def grad(teach_score, stud_score):
        teach = jnp.exp2(teach_score * (LOG2E / math.sqrt(TH)) - teach_log)
        stud = jnp.exp2(stud_score * (LOG2E / math.sqrt(SH)) - stud_log)
        return (weights * (stud - teach)).astype(BF16)

    def step(index, _):
        first, second, pack = key_chunk(keys_ref, index * chunk, chunk)
        left = grad(scores_of(span_ref[0], first), scores_of(span_ref[1], pack))
        right = grad(scores_of(span_ref[0], second), scores_of(span_ref[2], pack))
        mix = jnp.dot(left, span_ref[1], preferred_element_type=F32)
        mix = mix + jnp.dot(right, span_ref[2], preferred_element_type=F32)
        mix = (mix * (1.0 / math.sqrt(SH))).astype(key_ref.dtype)
        key_ref[pl.ds(index * chunk, chunk)] = mix.reshape(chunk, own, LANES)
        return 0

    lax.fori_loop(0, keys_ref.shape[0] // chunk, step, 0, unroll=True)


def unpack_keys(in_ref, out_ref):
    half = in_ref.shape[1]
    group = 16
    for start in range(0, in_ref.shape[0], group):
        for side in range(2):
            parts = [
                in_ref[head, :, side * HALF : side * HALF + SH].astype(F32)
                for head in range(start, start + group)
            ]
            out_ref[side * half : (side + 1) * half, start * SH : (start + group) * SH] = (
                jnp.concatenate(parts, axis=1)
            )


def unpack_rows(near_ref, core_ref, mine_ref, along_ref, across_ref, out_ref, part_ref):
    spot = near_ref[0] * CORES + core_ref[0]
    part_ref[spot] = mine_ref[0]
    part_ref[spot ^ 2] = along_ref[0]
    part_ref[spot ^ 1] = across_ref[0]
    part_ref[spot ^ 3] = across_ref[1]
    out_ref[...] = jnp.concatenate(
        [part_ref[head, :, :SH] for head in range(part_ref.shape[0])], axis=1
    )


def call(body, shapes, scratch=(), smem=0, raw=0, raw_out=0, flops=0, room=48):
    kinds = [pltpu.SMEM, pltpu.HBM, pltpu.VMEM]
    specs = lambda counts: [
        pl.BlockSpec(memory_space=kind) for kind, count in zip(kinds, counts) for _ in range(count)
    ]

    def run(*args):
        many = isinstance(shapes, (list, tuple))
        outs = specs((0, raw_out, (len(shapes) if many else 1) - raw_out))
        moved = sum(arg.size * arg.dtype.itemsize for arg in args)
        return pl.pallas_call(
            body,
            out_shape=shapes,
            in_specs=specs((smem, raw, len(args) - smem - raw)),
            out_specs=outs if many else outs[0],
            scratch_shapes=list(scratch),
            cost_estimate=pl.CostEstimate(flops=flops, bytes_accessed=moved, transcendentals=0),
            compiler_params=pltpu.CompilerParams(vmem_limit_bytes=room * 2**20),
        )(*args)

    return run


def on_device(teacher_span, teacher_context, student_span, student_context, query_weights):
    groups, tps = lax.axis_size("group"), lax.axis_size("tp")
    heads = tps * NEAR * CORES
    near = NEAR * CORES
    rows_own, tokens_own = teacher_span.shape[0], teacher_context.shape[0]
    half = tokens_own // 2
    queries = query_weights.shape[0]
    shape = jax.ShapeDtypeStruct

    def trade(array, axes):
        return lax.all_to_all(array, axes, split_axis=0, concat_axis=0, tiled=True)

    core = lax.axis_index("core").astype(jnp.int32)
    side = core.reshape(1)
    spot = lax.axis_index("near").astype(jnp.int32).reshape(1)
    piece = shape(((NEAR + 1) * rows_own, LANES), BF16)
    keys, kept, given = call(
        pack,
        (shape((heads, 3 * half, LANES), BF16), piece, piece),
        scratch=[
            pltpu.VMEM(teacher_span.shape, BF16),
            pltpu.VMEM(teacher_context.shape, BF16),
            pltpu.VMEM(student_span.shape, BF16),
            pltpu.VMEM(student_context.shape, BF16),
            pltpu.VMEM((heads, 3 * half, LANES), BF16),
            pltpu.SemaphoreType.DMA((8,)),
        ],
        smem=1,
        raw=4,
        raw_out=1,
        room=62,
    )(
        spot ^ side,
        teacher_span,
        teacher_context,
        student_span,
        student_context,
    )
    other = lax.ppermute(given, "core", [(0, 1), (1, 0)])
    order = lambda first, second: jnp.stack(
        [part.reshape(NEAR + 1, rows_own, LANES) for part in (first, second)], axis=1
    )
    shard = jnp.where(core == 0, order(kept, other), order(other, kept))
    shard = shard.reshape(1, (NEAR + 1) * CORES * rows_own, LANES)
    keys = trade(keys, ("tp", "near", "core"))
    rows = lax.all_gather(
        shard,
        ("group", "near", "core"),
        axis=0,
        tiled=True,
        axis_index_groups=[
            [z * CORES + (z + side) % CORES for z in range(groups * NEAR)] for side in range(CORES)
        ],
    )

    deep = queries // groups
    logs, spans = call(
        functools.partial(totals_kernel, 8, 32),
        (shape((groups, 3 * deep // 4 + 8, LANES), F32), shape((3, queries, LANES), BF16)),
        scratch=[pltpu.VMEM((4, heads * half, queries), F32)],
        smem=1,
        flops=2**31,
    )(spot, keys, rows)
    logs = trade(logs, "group")
    tokens_all = tokens_own * heads * groups
    weights = math.sqrt(tokens_all) * query_weights
    own = lax.dynamic_slice(weights, (lax.axis_index("group") * deep,), (deep,))
    own = jnp.broadcast_to(own[:, None], (deep, LANES))
    parts, mine = call(
        functools.partial(grads_kernel, 32),
        (shape((heads, half, LANES), BF16), shape((near, rows_own, LANES), F32)),
        scratch=[pltpu.VMEM((near, rows_own, LANES), F32)],
        smem=2,
        flops=2**30,
    )(spot, side, logs, weights.reshape(1, queries), own, keys, spans)
    parts = trade(parts, ("tp", "near", "core"))
    flip = lambda array, axis: lax.ppermute(array, axis, [(0, 1), (1, 0)])
    along = flip(mine[CORES:], "near")
    across = flip(jnp.stack([mine[1], along[1]]), "core")
    grad_span = call(
        unpack_rows,
        shape((rows_own, near * SH), F32),
        scratch=[pltpu.VMEM((near, rows_own, LANES), F32)],
        smem=2,
    )(spot, side, mine, along, across)
    grad_context = call(unpack_keys, shape((tokens_own, heads * SH), F32))(parts)
    return (grad_span, grad_context)


def solution(mesh):
    ctx, tp = mesh.devices.shape
    split = Mesh(
        mesh.devices.reshape(ctx // (NEAR * CORES), NEAR, CORES, tp),
        ("group", "near", "core", "tp"),
    )
    rows = ("group", "near", "core")
    tokens = rows + ("tp",)
    placed = (P(rows, "tp"), P(tokens, None), P(rows, "tp"), P(tokens, None), P())
    return jax.shard_map(
        on_device,
        mesh=split,
        in_specs=placed,
        out_specs=(P(rows, "tp"), P(tokens, None)),
        check_vma=False,
    )
```
